128 devices in a mesh: row: 16 (over y, x), col: 8 (over z, core).
Axes of the slice: x: 4, y: 4, z: 4, core: 2. Of those that a mesh axis runs over, the one named last changes fastest.
Arguments:
- hamilton: float32 [24576, 24576], P('row', 'col'), as said below
- start_block: float32 [48, 24576], P(None, 'col'), may hold values from -6 to 6
- bounds: float32 [3], replicated, as said below
- degree_pick: int32 [48], replicated, may hold values from 0 to 1
Outputs:
- basis: float32 [48, 24576], P(None, 'col')
The draws below stay inside these ranges and needn't reach their ends.
Inputs may be any that keep to these rules, and one draw needn't show every extreme that they name: hamilton is symmetric and all its eigenvalues lie between bounds[0] and bounds[2]. bounds[0] < bounds[1] < bounds[2].
All inputs are finite; a program needn't handle non-finite values.
Results may differ from the reference program's by a relative error of at most 0.0003.
Values sent between devices are 32-bit elements; how exact they have to be, the bound alone decides.
A program may use at most 128 MiB of HBM per device.

```python
import jax
import jax.numpy as jnp
from jax import lax

NEV = 48
DLO = 6
DHI = 10
N = 24576


def draw_hamilton(key, part):
    key = jax.random.fold_in(key, 11)
    raw = jax.random.normal(key, (N, N), jnp.float32)
    return (raw + raw.T) * (0.5 / jnp.sqrt(2.0 * N))


def draw_bounds(key, part):
    key = jax.random.fold_in(key, 23)
    unit = jax.random.uniform(key, (3,), jnp.float32)
    lowest = -1.25 + 0.13 * unit[0]
    lower_end = -0.5 + 0.2 * unit[1]
    upper_end = 1.08 + 0.12 * unit[2]
    return jnp.stack([lowest, lower_end, upper_end]).astype(jnp.float32)


def place_ends(drawn, key, smallest, top_value):
    longest = drawn.shape.index(max(drawn.shape))
    spots = []
    for shift in (0, 1):
        where = [jax.random.randint(jax.random.fold_in(key, axis), (), 0, length) for axis, length in enumerate(drawn.shape)]
        where[longest] = (where[longest] + shift) % drawn.shape[longest]
        spots.append(tuple(where))
    return drawn.at[spots[0]].set(smallest).at[spots[1]].set(top_value)


def levels(own_key, shape, cuts, smallest, largest):
    factor_of = 1.0
    for axis_at, parts in cuts:
        heights = jax.random.uniform(jax.random.fold_in(jax.random.fold_in(own_key, 6), axis_at), (parts,), jnp.float32, smallest / len(cuts), largest / len(cuts))
        factor_of = factor_of * jnp.repeat(jnp.exp(heights), shape[axis_at] // parts).reshape((-1,) + (1,) * (len(shape) - 1 - axis_at))
    return factor_of


def gaussian(stream_key, extent, spread, bound, shards=(), held_as=jnp.bfloat16):
    values = spread * jax.random.normal(stream_key, extent, jnp.float32)
    if shards:
        values = values * levels(stream_key, extent, shards, -0.22, 0.18)
    return jnp.clip(values, -bound, bound).astype(held_as)


def setup_inputs(seed: int = 0) -> dict:
    splits = jax.random.split(jax.random.key(seed), 5)
    hamilton = draw_hamilton(jax.random.fold_in(splits[4], 71), 0)
    start_block = gaussian(splits[1], (NEV, N), 1.0, 6.0, ((1, 8),), jnp.float32)
    bounds = draw_bounds(jax.random.fold_in(splits[4], 71), 0)
    degree_pick = place_ends(jax.random.randint(splits[3], (NEV,), 0, 2), jax.random.fold_in(splits[3], 1), 0, 1).astype(jnp.int32)
    return dict(hamilton=hamilton, start_block=start_block, bounds=bounds, degree_pick=degree_pick)


def apply_shifted(block, hamilton, shift):
    return jnp.dot(block, hamilton, precision=lax.Precision.HIGHEST) - shift * block

def cholesky_step(block):
    gram = jnp.dot(block, block.T, precision=lax.Precision.HIGHEST)
    lower_factor = jnp.linalg.cholesky(gram)
    return lax.linalg.triangular_solve(lower_factor, block, left_side=True, lower=True)

def reference(hamilton, start_block, bounds, degree_pick):
    lowest = bounds[0]
    lower_end = bounds[1]
    upper_end = bounds[2]
    half_width = (upper_end - lower_end) / 2.0
    center = (upper_end + lower_end) / 2.0
    sigma_one = half_width / (lowest - center)
    sigma = sigma_one
    previous = jnp.zeros_like(start_block)
    current = start_block
    scale = sigma_one / half_width
    coeff = jnp.float32(0.0) * sigma
    kept = start_block
    for step in range(1, DHI + 1):
        if step > 1:
            new_sigma = 1.0 / (2.0 / sigma_one - sigma)
            scale = 2.0 * new_sigma / half_width
            coeff = sigma * new_sigma
            sigma = new_sigma
        following = scale * apply_shifted(current, hamilton, center) - coeff * previous
        previous, current = (current, following)
        if step == DLO:
            kept = current
    filtered = jnp.where(degree_pick[:, None] == 0, kept, current)
    first = cholesky_step(filtered)
    second = cholesky_step(first)
    return second * jnp.sqrt(jnp.float32(N))
```

```python
import functools

import jax
import jax.numpy as jnp
from jax import lax
from jax.experimental import pallas as pl
from jax.experimental.pallas import tpu as pltpu
from jax.sharding import PartitionSpec as P

DLO = 6
DHI = 10
NEV = 48
LANES = 128
SUB = 8
TPB = NEV // SUB
MESH = pl.DeviceIdType.MESH
NT = (((1,), (1,)), ((), ()))
NN = (((1,), (0,)), ((), ()))
FAR_FIRST = (2, 1, 3, 0)
F32 = jnp.float32
BF16 = jnp.bfloat16


def split_planes(value):
    high = value.astype(BF16)
    low = (value - high.astype(F32)).astype(BF16)
    return high, low


def fold(product):
    return product[:NEV] + product[NEV:]


def kernel(
    sizes,
    ham_ref, start_ref, bounds_ref, pick_ref, out_ref,
    stage, high_ref, low_ref, planes, chunk_planes, filtered_ref,
    part_o, part_e, land_o, land_e, vec_o, vec_e, last_o, last_e, kept_ref,
    pick_tiles, gram_a, gram_b, work,
    ham_sem,
    rs_o_s, rs_o_r, ag_o_s, ag_o_r, rs_e_s, rs_e_r, ag_e_s, ag_e_r, g_s, g_r, h_s, h_r,
):
    rows_dev, cols_dev = sizes
    row = lax.axis_index("row")
    col = lax.axis_index("col")
    y, x = row // 4, lax.rem(row, 4)
    z, core = col // 2, lax.rem(col, 2)
    blocks_o, blocks_e = rows_dev // LANES, cols_dev // LANES
    own_o = blocks_o * TPB // 8
    own_e = blocks_e * TPB // 16
    grp_o = rows_dev // 4
    grp_e = cols_dev // 4

    peers_o = [(dz, dc) for dz in FAR_FIRST for dc in (0, 1) if (dz, dc) != (0, 0)]
    peers_e = [(dy, dx) for dy in FAR_FIRST for dx in FAR_FIRST if (dy, dx) != (0, 0)]

    def index_o(offset):
        return lax.rem(z + offset[0], 4) * 2 + lax.rem(core + offset[1], 2)

    def index_e(offset):
        return lax.rem(y + offset[0], 4) * 4 + lax.rem(x + offset[1], 4)

    def tiles_o(index):
        return pl.ds(index * own_o, own_o)

    def tiles_e(index):
        return pl.ds(index * own_e, own_e)

    def scatter_o(slot):
        to = index_o(peers_o[slot])
        return pltpu.make_async_remote_copy(
            src_ref=part_o.at[tiles_o(to)], dst_ref=land_o.at[slot],
            send_sem=rs_o_s.at[slot], recv_sem=rs_o_r.at[slot],
            device_id=(row, to), device_id_type=MESH)

    def scatter_e(slot):
        to = index_e(peers_e[slot])
        return pltpu.make_async_remote_copy(
            src_ref=part_e.at[tiles_e(to)], dst_ref=land_e.at[slot],
            send_sem=rs_e_s.at[slot], recv_sem=rs_e_r.at[slot],
            device_id=(to, col), device_id_type=MESH)

    def gather_o(slot):
        mine = vec_o.at[tiles_o(col)]
        return pltpu.make_async_remote_copy(
            src_ref=mine, dst_ref=mine,
            send_sem=ag_o_s.at[slot], recv_sem=ag_o_r.at[slot],
            device_id=(row, index_o(peers_o[slot])), device_id_type=MESH)

    def gather_e(slot):
        mine = vec_e.at[tiles_e(row)]
        return pltpu.make_async_remote_copy(
            src_ref=mine, dst_ref=mine,
            send_sem=ag_e_s.at[slot], recv_sem=ag_e_r.at[slot],
            device_id=(index_e(peers_e[slot]), col), device_id_type=MESH)

    def gram_copy(buffer, send, recv, slot):
        return pltpu.make_async_remote_copy(
            src_ref=buffer.at[col], dst_ref=buffer.at[col],
            send_sem=send.at[slot], recv_sem=recv.at[slot],
            device_id=(row, index_o(peers_o[slot])), device_id_type=MESH)

    def ham_copy(place):
        at = lax.rem(z + FAR_FIRST[place], 4) * grp_o
        return pltpu.make_async_copy(
            ham_ref.at[pl.ds(pl.multiple_of(at, LANES), grp_o)], stage.at[place], ham_sem.at[place])

    for place in range(4):
        ham_copy(place).start()

    barrier = pltpu.get_barrier_semaphore()
    for offset in peers_o:
        pl.semaphore_signal(barrier, inc=1, device_id=(row, index_o(offset)), device_id_type=MESH)
    for offset in peers_e:
        pl.semaphore_signal(barrier, inc=1, device_id=(index_e(offset), col), device_id_type=MESH)
    pl.semaphore_wait(barrier, len(peers_o) + len(peers_e))

    lowest = jnp.full((SUB, LANES), bounds_ref[0], F32)
    lower_end = jnp.full((SUB, LANES), bounds_ref[1], F32)
    upper_end = jnp.full((SUB, LANES), bounds_ref[2], F32)
    half_width = (upper_end - lower_end) / 2.0
    center = (upper_end + lower_end) / 2.0
    sigma_one = half_width / (lowest - center)

    vector_at = lax.broadcasted_iota(jnp.int32, (TPB, SUB, LANES), 0) * SUB + lax.broadcasted_iota(
        jnp.int32, (TPB, SUB, LANES), 1)
    picked = jnp.zeros((TPB, SUB, LANES), jnp.int32)
    for v in range(NEV):
        picked = jnp.where(vector_at == v, pick_ref[v], picked)
    pick_tiles[...] = picked
    gram_a[...] = jnp.zeros_like(gram_a)
    gram_b[...] = jnp.zeros_like(gram_b)

    for b in range(blocks_e):
        value = start_ref[:, b * LANES:(b + 1) * LANES]
        high, low = split_planes(value)
        planes[0:NEV, b * LANES:(b + 1) * LANES] = high
        planes[NEV:2 * NEV, b * LANES:(b + 1) * LANES] = low
        vec_e[b * TPB:(b + 1) * TPB] = value.reshape(TPB, SUB, LANES)
    last_e[...] = vec_e[tiles_e(row)]
    last_o[...] = jnp.zeros_like(last_o)

    offset = row * rows_dev - col * cols_dev
    inside = (offset >= 0) & (offset < cols_dev)
    diag_at = jnp.where(inside, offset, 0)
    diag_weight = jnp.where(inside, 1.0, 0.0).astype(F32)
    eye = (lax.broadcasted_iota(jnp.int32, (LANES, LANES), 0)
           == lax.broadcasted_iota(jnp.int32, (LANES, LANES), 1))
    shift = jnp.where(eye, center[0:1] * diag_weight, 0.0)

    def store_tiles(part, first_tile, total, blocks, add):
        for b in range(blocks):
            tile = total[:, b * LANES:(b + 1) * LANES].reshape(TPB, SUB, LANES)
            at = pl.ds(first_tile + b * TPB, TPB)
            if add:
                tile = tile + part[at]
            part[at] = tile

    def to_planes(vec, first_tile, blocks):
        for b in range(blocks):
            value = vec[pl.ds(first_tile + b * TPB, TPB)].reshape(NEV, LANES)
            high, low = split_planes(value)
            chunk_planes[0:NEV, b * LANES:(b + 1) * LANES] = high
            chunk_planes[NEV:2 * NEV, b * LANES:(b + 1) * LANES] = low

    def slots_o(dz):
        return [s for s, p in enumerate(peers_o) if p[0] == dz]

    def slots_e(dy):
        return [s for s, p in enumerate(peers_e) if p[0] == dy]

    for place, dz in enumerate(FAR_FIRST):
        group = lax.rem(z + dz, 4)
        ham_copy(place).wait()
        for b in range(grp_o // LANES):
            at = pl.ds(pl.multiple_of(diag_at + group * grp_o + b * LANES, LANES), LANES)
            rows_at = slice(b * LANES, (b + 1) * LANES)
            stage[place, rows_at, at] = stage[place, rows_at, at] - shift

        def split_rows(i, carry):
            from_row = pl.multiple_of(i * 16, 16)
            high, low = split_planes(stage[place, pl.ds(from_row, 16), :])
            to_row = pl.multiple_of(group * grp_o + i * 16, 16)
            high_ref[pl.ds(to_row, 16), :] = high
            low_ref[pl.ds(to_row, 16), :] = low
            return carry

        lax.fori_loop(0, grp_o // 16, split_rows, 0)
        rows_at = pl.ds(pl.multiple_of(group * grp_o, LANES), grp_o)
        total = fold(
            lax.dot_general(planes[...], high_ref[rows_at, :], NT, preferred_element_type=F32)
            + lax.dot_general(planes[...], low_ref[rows_at, :], NT, preferred_element_type=F32))
        store_tiles(part_o, group * (grp_o // LANES * TPB), total, grp_o // LANES, False)
        for slot in slots_o(dz):
            scatter_o(slot).start()

    def reduce_o(scale, coeff):
        for slot in range(len(peers_o)):
            scatter_o(slot).wait_recv()
        total = part_o[tiles_o(col)]
        for slot in range(len(peers_o)):
            total = total + land_o[slot]
        value = scale * total - coeff * last_o[...]
        last_o[...] = value
        vec_o[tiles_o(col)] = value
        for slot in range(len(peers_o)):
            gather_o(slot).start()
        for slot in range(len(peers_o)):
            scatter_o(slot).wait_send()

    def reduce_e(scale, coeff):
        for slot in range(len(peers_e)):
            scatter_e(slot).wait_recv()
        total = part_e[tiles_e(row)]
        for slot in range(len(peers_e)):
            total = total + land_e[slot]
        value = scale * total - coeff * last_e[...]
        last_e[...] = value
        return value

    def spread_e(value):
        vec_e[tiles_e(row)] = value
        for slot in range(len(peers_e)):
            gather_e(slot).start()
        for slot in range(len(peers_e)):
            scatter_e(slot).wait_send()

    def product_e():
        width = grp_o // LANES
        for turn, dz in enumerate(FAR_FIRST):
            for slot in slots_o(dz):
                gather_o(slot).wait_recv()
            group = lax.rem(z + 4 - dz, 4)
            to_planes(vec_o, group * (width * TPB), width)
            left = chunk_planes[:, 0:grp_o]
            rows_at = pl.ds(pl.multiple_of(group * grp_o, LANES), grp_o)
            for dy in FAR_FIRST:
                target = lax.rem(y + dy, 4)
                cols_at = pl.ds(pl.multiple_of(target * grp_e, LANES), grp_e)
                total = fold(
                    lax.dot_general(left, high_ref[rows_at, cols_at], NN, preferred_element_type=F32)
                    + lax.dot_general(left, low_ref[rows_at, cols_at], NN, preferred_element_type=F32))
                store_tiles(part_e, target * (grp_e // LANES * TPB), total, grp_e // LANES, turn > 0)
                if turn == 3:
                    for slot in slots_e(dy):
                        scatter_e(slot).start()
        for slot in range(len(peers_o)):
            gather_o(slot).wait_send()

    def product_o():
        width = grp_e // LANES
        for turn, dy in enumerate(FAR_FIRST):
            for slot in slots_e(dy):
                gather_e(slot).wait_recv()
            group = lax.rem(y + 4 - dy, 4)
            to_planes(vec_e, group * (width * TPB), width)
            left = chunk_planes[:, 0:grp_e]
            cols_at = pl.ds(pl.multiple_of(group * grp_e, LANES), grp_e)
            for dz in FAR_FIRST:
                target = lax.rem(z + dz, 4)
                rows_at = pl.ds(pl.multiple_of(target * grp_o, LANES), grp_o)
                total = fold(
                    lax.dot_general(left, high_ref[rows_at, cols_at], NT, preferred_element_type=F32)
                    + lax.dot_general(left, low_ref[rows_at, cols_at], NT, preferred_element_type=F32))
                store_tiles(part_o, target * (grp_o // LANES * TPB), total, grp_o // LANES, turn > 0)
                if turn == 3:
                    for slot in slots_o(dz):
                        scatter_o(slot).start()
        for slot in range(len(peers_e)):
            gather_e(slot).wait_send()

    def next_sigma(sigma):
        new_sigma = 1.0 / (2.0 / sigma_one - sigma)
        return 2.0 * new_sigma / half_width, sigma * new_sigma, new_sigma

    reduce_o(sigma_one / half_width, 0.0 * sigma_one)

    def two_steps(pair, sigma):
        scale, coeff, sigma = next_sigma(sigma)
        product_e()
        value = reduce_e(scale, coeff)
        kept_ref[...] = value * jnp.where(pair == DLO // 2 - 1, 1.0, 0.0) + jnp.where(
            pair == DLO // 2 - 1, jnp.zeros_like(value), kept_ref[...])
        spread_e(value)
        scale, coeff, sigma = next_sigma(sigma)
        product_o()
        reduce_o(scale, coeff)
        return sigma

    kept_ref[...] = jnp.zeros_like(kept_ref)
    sigma = lax.fori_loop(0, DHI // 2 - 1, two_steps, sigma_one)
    scale, coeff, sigma = next_sigma(sigma)
    product_e()
    value = reduce_e(scale, coeff)
    kept_ref[...] = jnp.where(
        jnp.stack([pick_tiles[lax.rem(row * own_e + t, TPB)] for t in range(own_e)]) == 0,
        kept_ref[...], value)
    spread_e(kept_ref[...])

    for dy in FAR_FIRST:
        for slot in slots_e(dy):
            gather_e(slot).wait_recv()
    for b in range(blocks_e):
        filtered_ref[:, b * LANES:(b + 1) * LANES] = vec_e[b * TPB:(b + 1) * TPB].reshape(NEV, LANES)
    for slot in range(len(peers_e)):
        gather_e(slot).wait_send()

    lane = lax.broadcasted_iota(jnp.int32, (NEV, LANES), 1)
    sublane = lax.broadcasted_iota(jnp.int32, (NEV, LANES), 0)

    def inverse_factor(buffer, send, recv):
        value = filtered_ref[...]
        gram = lax.dot_general(value, value, NT, precision=lax.Precision.HIGHEST, preferred_element_type=F32)
        buffer[col, :, 0:NEV] = gram
        for slot in range(len(peers_o)):
            gram_copy(buffer, send, recv, slot).start()
        for slot in range(len(peers_o)):
            gram_copy(buffer, send, recv, slot).wait()
        total = buffer[0]
        for i in range(1, 8):
            total = total + buffer[i]
        work[...] = jnp.where(lane < NEV, total, jnp.where(lane - NEV == sublane, 1.0, 0.0))

        def eliminate(j, carry):
            pivot_row = work[pl.ds(j, 1), :]
            pivot = jnp.sum(jnp.where(lane[0:1] == j, pivot_row, 0.0), axis=1, keepdims=True)
            column = jnp.sum(jnp.where(lane == j, work[...], 0.0), axis=1, keepdims=True)
            factor = jnp.where(sublane[:, 0:1] > j, column / pivot, 0.0)
            scaled = pivot_row * lax.rsqrt(pivot)
            updated = work[...] - factor * pivot_row
            work[...] = jnp.where(sublane == j, scaled, updated)
            return carry

        lax.fori_loop(0, NEV, eliminate, 0)
        return work[:, NEV:2 * NEV]

    first = jnp.dot(inverse_factor(gram_a, g_s, g_r), filtered_ref[...],
                    precision=lax.Precision.HIGHEST, preferred_element_type=F32)
    filtered_ref[...] = first
    order = jnp.sqrt(jnp.full((NEV, NEV), 8 * cols_dev, F32))
    out_ref[...] = jnp.dot(order * inverse_factor(gram_b, h_s, h_r), filtered_ref[...],
                           precision=lax.Precision.HIGHEST, preferred_element_type=F32)


def on_device(hamilton, start_block, bounds, degree_pick):
    rows_dev, cols_dev = hamilton.shape
    tiles_o = rows_dev // LANES * TPB
    tiles_e = cols_dev // LANES * TPB
    own_o, own_e = tiles_o // 8, tiles_e // 16
    vmem = pltpu.VMEM
    dma = pltpu.SemaphoreType.DMA
    return pl.pallas_call(
        functools.partial(kernel, (rows_dev, cols_dev)),
        out_shape=jax.ShapeDtypeStruct((NEV, cols_dev), F32),
        in_specs=[
            pl.BlockSpec(memory_space=pl.ANY),
            pl.BlockSpec(memory_space=pltpu.VMEM),
            pl.BlockSpec(memory_space=pltpu.SMEM),
            pl.BlockSpec(memory_space=pltpu.SMEM),
        ],
        out_specs=pl.BlockSpec(memory_space=pltpu.VMEM),
        scratch_shapes=[
            vmem((4, rows_dev // 4, cols_dev), F32),
            vmem((rows_dev, cols_dev), BF16),
            vmem((rows_dev, cols_dev), BF16),
            vmem((2 * NEV, cols_dev), BF16),
            vmem((2 * NEV, cols_dev // 4), BF16),
            vmem((NEV, cols_dev), F32),
            vmem((tiles_o, SUB, LANES), F32),
            vmem((tiles_e, SUB, LANES), F32),
            vmem((7, own_o, SUB, LANES), F32),
            vmem((15, own_e, SUB, LANES), F32),
            vmem((tiles_o, SUB, LANES), F32),
            vmem((tiles_e, SUB, LANES), F32),
            vmem((own_o, SUB, LANES), F32),
            vmem((own_e, SUB, LANES), F32),
            vmem((own_e, SUB, LANES), F32),
            vmem((TPB, SUB, LANES), jnp.int32),
            vmem((8, NEV, LANES), F32),
            vmem((8, NEV, LANES), F32),
            vmem((NEV, LANES), F32),
            dma((4,)),
            dma((7,)), dma((7,)), dma((7,)), dma((7,)),
            dma((15,)), dma((15,)), dma((15,)), dma((15,)),
            dma((7,)), dma((7,)), dma((7,)), dma((7,)),
        ],
        compiler_params=pltpu.CompilerParams(
            collective_id=0, has_side_effects=True, vmem_limit_bytes=56 * 2**20),
        cost_estimate=pl.CostEstimate(
            flops=2 * DHI * 4 * NEV * rows_dev * cols_dev,
            bytes_accessed=4 * rows_dev * cols_dev, transcendentals=0),
    )(hamilton, start_block, bounds, degree_pick)


def solution(mesh):
    in_specs = (P("row", "col"), P(None, "col"), P(), P())
    out_specs = P(None, "col")
    return jax.shard_map(
        on_device, mesh=mesh, in_specs=in_specs, out_specs=out_specs, check_vma=False
    )
```

```python
import functools

import jax
import jax.numpy as jnp
from jax import lax
from jax.experimental import pallas as pl
from jax.experimental.pallas import tpu as pltpu
from jax.sharding import PartitionSpec as P

DLO = 6
DHI = 10
NEV = 48
GROUPS = 2
GV = NEV // GROUPS
PADV = 32
LANES = 128
SUB = 8
TPB = GV // SUB
PAIR = 9
FIVE = 5
FOUR = 4
CHUNK = 256
SLOTS = 4
MESH = pl.DeviceIdType.MESH
NT = (((1,), (1,)), ((), ()))
NN = (((1,), (0,)), ((), ()))
FAR_FIRST = (2, 1, 3, 0)
F32 = jnp.float32
BF16 = jnp.bfloat16


def split_planes(value):
    high = value.astype(BF16)
    low = (value - high.astype(F32)).astype(BF16)
    return high, low


def kernel(
    sizes,
    ham_ref, start_ref, bounds_ref, pick_ref, out_ref,
    stage, high_ref, low_ref, high_t, low_t, planes, group_planes, filtered_ref,
    part_o, part_e, land_o, land_e, vec_o, vec_e, last_o, last_e, kept_ref,
    pick_tiles, gram_a, gram_b, work,
    ham_sem,
    rs_o_s, rs_o_r, ag_o_s, ag_o_r, rs_e_s, rs_e_r, ag_e_s, ag_e_r,
    ax_o_s, ax_o_r, ax_e_s, ax_e_r, g_s, g_r, h_s, h_r,
):
    rows_dev, cols_dev = sizes
    row = lax.axis_index("row")
    col = lax.axis_index("col")
    y, x = row // 4, lax.rem(row, 4)
    z, core = col // 2, lax.rem(col, 2)
    blocks_o, blocks_e = rows_dev // LANES, cols_dev // LANES
    wide = cols_dev // 4
    wide_tiles = wide // LANES * TPB
    odd_row = lax.rem(row, 2)

    peers_o = [(dz, dc) for dz in FAR_FIRST for dc in (0, 1) if (dz, dc) != (0, 0)]
    peers_e = [(dy, dx) for dy in FAR_FIRST for dx in FAR_FIRST if (dy, dx) != (0, 0)]
    all_o, all_e = range(len(peers_o)), range(len(peers_e))

    def index_o(offset):
        return lax.rem(z + offset[0], 4) * 2 + lax.rem(core + offset[1], 2)

    def index_e(offset):
        return lax.rem(y + offset[0], 4) * 4 + lax.rem(x + offset[1], 4)

    def summed(index):
        return pl.ds((index // 2) * PAIR + lax.rem(index, 2) * FOUR, FIVE)

    def four(index):
        return pl.ds((index // 2) * PAIR + lax.rem(index, 2) * FIVE, FOUR)

    def fifth(index):
        return pl.ds((index // 2) * PAIR + FOUR, 1)

    def scatter_o(g, slot):
        to = index_o(peers_o[slot])
        return pltpu.make_async_remote_copy(
            src_ref=part_o.at[g, summed(to)], dst_ref=land_o.at[g, slot],
            send_sem=rs_o_s.at[g, slot], recv_sem=rs_o_r.at[g, slot],
            device_id=(row, to), device_id_type=MESH)

    def scatter_e(g, slot):
        to = index_e(peers_e[slot])
        return pltpu.make_async_remote_copy(
            src_ref=part_e.at[g, summed(to)], dst_ref=land_e.at[g, slot],
            send_sem=rs_e_s.at[g, slot], recv_sem=rs_e_r.at[g, slot],
            device_id=(to, col), device_id_type=MESH)

    def gather_o(g, slot, extra):
        mine = vec_o.at[g, fifth(col) if extra else four(col)]
        send, recv = (ax_o_s, ax_o_r) if extra else (ag_o_s, ag_o_r)
        return pltpu.make_async_remote_copy(
            src_ref=mine, dst_ref=mine, send_sem=send.at[g, slot], recv_sem=recv.at[g, slot],
            device_id=(row, index_o(peers_o[slot])), device_id_type=MESH)

    def gather_e(g, slot, extra):
        mine = vec_e.at[g, fifth(row) if extra else four(row)]
        send, recv = (ax_e_s, ax_e_r) if extra else (ag_e_s, ag_e_r)
        return pltpu.make_async_remote_copy(
            src_ref=mine, dst_ref=mine, send_sem=send.at[g, slot], recv_sem=recv.at[g, slot],
            device_id=(index_e(peers_e[slot]), col), device_id_type=MESH)

    def spread(vec, g, value, index, odd, gather, slots):
        @pl.when(odd == 0)
        def _():
            vec[g, pl.ds((index // 2) * PAIR, FIVE)] = value
            for slot in slots:
                gather(g, slot, False).start()
                gather(g, slot, True).start()

        @pl.when(odd == 1)
        def _():
            vec[g, pl.ds((index // 2) * PAIR + FIVE, FOUR)] = value[1:]
            for slot in slots:
                gather(g, slot, False).start()

    def arrived(g, odd, gather, peers):
        for slot in range(len(peers)):
            gather(g, slot, False).wait_recv()

        @pl.when(odd == 0)
        def _():
            for slot, offset in enumerate(peers):
                if offset[1] % 2 == 0:
                    gather(g, slot, True).wait_recv()

        @pl.when(odd == 1)
        def _():
            for slot, offset in enumerate(peers):
                if offset[1] % 2 == 1:
                    gather(g, slot, True).wait_recv()

    def left(g, odd, gather, slots):
        for slot in slots:
            gather(g, slot, False).wait_send()

        @pl.when(odd == 0)
        def _():
            for slot in slots:
                gather(g, slot, True).wait_send()

    def gram_copy(buffer, send, recv, slot):
        return pltpu.make_async_remote_copy(
            src_ref=buffer.at[col], dst_ref=buffer.at[col],
            send_sem=send.at[slot], recv_sem=recv.at[slot],
            device_id=(row, index_o(peers_o[slot])), device_id_type=MESH)

    chunks = rows_dev // CHUNK

    def chunk_at(place):
        half = lax.rem(z // 2 + 1 + place // (chunks // 2), 2)
        return pl.multiple_of(half * wide + place % (chunks // 2) * CHUNK, CHUNK)

    def ham_copy(place):
        return pltpu.make_async_copy(
            ham_ref.at[pl.ds(chunk_at(place), CHUNK)], stage.at[place % SLOTS], ham_sem.at[place % SLOTS])

    for place in range(SLOTS):
        ham_copy(place).start()

    barrier = pltpu.get_barrier_semaphore()
    for offset in peers_o:
        pl.semaphore_signal(barrier, inc=1, device_id=(row, index_o(offset)), device_id_type=MESH)
    for offset in peers_e:
        pl.semaphore_signal(barrier, inc=1, device_id=(index_e(offset), col), device_id_type=MESH)

    lowest = jnp.full((SUB, LANES), bounds_ref[0], F32)
    lower_end = jnp.full((SUB, LANES), bounds_ref[1], F32)
    upper_end = jnp.full((SUB, LANES), bounds_ref[2], F32)
    half_width = (upper_end - lower_end) / 2.0
    center = (upper_end + lower_end) / 2.0
    sigma_one = half_width / (lowest - center)

    tile_shape = (NEV // SUB, SUB, LANES)
    vector_at = lax.broadcasted_iota(jnp.int32, tile_shape, 0) * SUB + lax.broadcasted_iota(
        jnp.int32, tile_shape, 1)
    picked = jnp.zeros(tile_shape, jnp.int32)
    for v in range(NEV):
        picked = jnp.where(vector_at == v, pick_ref[v], picked)
    pick_tiles[...] = picked
    gram_a[...] = jnp.zeros_like(gram_a)
    gram_b[...] = jnp.zeros_like(gram_b)

    for b in range(blocks_e):
        value = start_ref[:, b * LANES:(b + 1) * LANES]
        high, low = split_planes(value)
        planes[0:NEV, b * LANES:(b + 1) * LANES] = high
        planes[NEV:2 * NEV, b * LANES:(b + 1) * LANES] = low
        for g in range(GROUPS):
            vec_e[g, b * TPB:(b + 1) * TPB] = value[g * GV:(g + 1) * GV].reshape(TPB, SUB, LANES)
    for g in range(GROUPS):
        last_e[g] = vec_e[g, summed(row)]
    last_o[...] = jnp.zeros_like(last_o)

    offset = row * rows_dev - col * cols_dev
    inside = (offset >= 0) & (offset < cols_dev)
    diag_at = jnp.where(inside, offset, 0)
    diag_weight = jnp.where(inside, 1.0, 0.0).astype(F32)
    eye = (lax.broadcasted_iota(jnp.int32, (LANES, LANES), 0)
           == lax.broadcasted_iota(jnp.int32, (LANES, LANES), 1))
    shift = jnp.where(eye, center[0:1] * diag_weight, 0.0)

    def store_tiles(part, g, first_tile, total):
        for b in range(total.shape[1] // LANES):
            part[g, pl.ds(first_tile + b * TPB, TPB)] = total[:, b * LANES:(b + 1) * LANES].reshape(
                TPB, SUB, LANES)

    for place in range(chunks):
        slot = place % SLOTS
        ham_copy(place).wait()
        first_row = chunk_at(place)
        for b in range(CHUNK // LANES):
            at = pl.ds(pl.multiple_of(diag_at + first_row + b * LANES, LANES), LANES)
            rows_at = slice(b * LANES, (b + 1) * LANES)
            stage[slot, rows_at, at] = stage[slot, rows_at, at] - shift

        def split_rows(i, carry):
            high, low = split_planes(stage[slot, pl.ds(pl.multiple_of(i * 16, 16), 16), :])
            to_row = pl.multiple_of(first_row + i * 16, 16)
            high_ref[pl.ds(to_row, 16), :] = high
            low_ref[pl.ds(to_row, 16), :] = low
            return carry

        lax.fori_loop(0, CHUNK // 16, split_rows, 0)
        if place + SLOTS < chunks:
            ham_copy(place + SLOTS).start()
        rows_at = pl.ds(first_row, CHUNK)
        total = (lax.dot_general(planes[...], high_ref[rows_at, :], NT, preferred_element_type=F32)
                 + lax.dot_general(planes[...], low_ref[rows_at, :], NT, preferred_element_type=F32))
        total = total[:NEV] + total[NEV:]
        for g in range(GROUPS):
            store_tiles(part_o, g, first_row // LANES * TPB, total[g * GV:(g + 1) * GV])
        if place == chunks // 2 - 1:
            pl.semaphore_wait(barrier, len(peers_o) + len(peers_e))

    def same_half(offset):
        return lax.rem(z + offset[0], 4) // 2 == z // 2

    for g in range(GROUPS):
        for slot in all_o:
            scatter_o(g, slot).start()

    def transpose(piece):
        rows_at = slice(piece * (rows_dev // 4), (piece + 1) * (rows_dev // 4))
        for j in range(0, cols_dev, 512):
            high_t[j:j + 512, rows_at] = high_ref[rows_at, j:j + 512].T
            low_t[j:j + 512, rows_at] = low_ref[rows_at, j:j + 512].T

    def reduce(g, scale, coeff, part, land, last, index, scatter, slots):
        for slot in slots:
            scatter(g, slot).wait_recv()
        total = part[g, summed(index)]
        for slot in slots:
            total = total + land[g, slot]
        value = scale * total - coeff * last[g]
        last[g] = value
        return value

    def reduce_o(g, scale, coeff):
        value = reduce(g, scale, coeff, part_o, land_o, last_o, col, scatter_o, all_o)
        spread(vec_o, g, value, col, core, gather_o, all_o)
        for slot in all_o:
            scatter_o(g, slot).wait_send()

    def reduce_e(g, scale, coeff):
        return reduce(g, scale, coeff, part_e, land_e, last_e, row, scatter_e, all_e)

    def spread_e(g, value):
        spread(vec_e, g, value, row, odd_row, gather_e, all_e)
        for slot in all_e:
            scatter_e(g, slot).wait_send()

    def to_planes(vec, g, blocks):
        nothing = jnp.zeros((PADV - GV, LANES), F32)
        for b in range(blocks):
            value = vec[g, b * TPB:(b + 1) * TPB].reshape(GV, LANES)
            high, low = split_planes(jnp.concatenate([value, nothing], axis=0))
            group_planes[0:PADV, b * LANES:(b + 1) * LANES] = high
            group_planes[PADV:2 * PADV, b * LANES:(b + 1) * LANES] = low

    def product(depth, high, low, target):
        cols_at = pl.ds(pl.multiple_of(target * wide, LANES), wide)
        vectors = group_planes[:, 0:depth]
        total = (lax.dot_general(vectors, high[:, cols_at], NN, preferred_element_type=F32)
                 + lax.dot_general(vectors, low[:, cols_at], NN, preferred_element_type=F32))
        return total[:GV] + total[PADV:PADV + GV]

    def product_e(g):
        arrived(g, core, gather_o, peers_o)
        to_planes(vec_o, g, blocks_o)
        for dy in FAR_FIRST:
            target = lax.rem(y + dy, 4)
            store_tiles(part_e, g, target * wide_tiles, product(rows_dev, high_ref, low_ref, target))
            for slot, offset in enumerate(peers_e):
                if offset[0] == dy:
                    scatter_e(g, slot).start()
        left(g, core, gather_o, all_o)

    def product_o(g):
        arrived(g, odd_row, gather_e, peers_e)
        to_planes(vec_e, g, blocks_e)
        for other in (1, 0):
            target = lax.rem(z // 2 + other, 2)
            store_tiles(part_o, g, target * wide_tiles, product(cols_dev, high_t, low_t, target))
            for slot, offset in enumerate(peers_o):
                @pl.when(same_half(offset) if other == 0 else jnp.logical_not(same_half(offset)))
                def _():
                    scatter_o(g, slot).start()
        left(g, odd_row, gather_e, all_e)

    def next_sigma(sigma):
        new_sigma = 1.0 / (2.0 / sigma_one - sigma)
        return 2.0 * new_sigma / half_width, sigma * new_sigma, new_sigma

    transpose(0)
    transpose(1)
    for g in range(GROUPS):
        reduce_o(g, sigma_one / half_width, 0.0 * sigma_one)
    transpose(2)
    transpose(3)

    def two_steps(pair, sigma):
        scale, coeff, sigma = next_sigma(sigma)
        for g in range(GROUPS):
            product_e(g)
        for g in range(GROUPS):
            value = reduce_e(g, scale, coeff)
            kept_ref[g] = jnp.where(pair == DLO // 2 - 1, value, kept_ref[g])
            spread_e(g, value)
        scale, coeff, sigma = next_sigma(sigma)
        for g in range(GROUPS):
            product_o(g)
        for g in range(GROUPS):
            reduce_o(g, scale, coeff)
        return sigma

    kept_ref[...] = jnp.zeros_like(kept_ref)
    sigma = lax.fori_loop(0, DHI // 2 - 1, two_steps, sigma_one)
    scale, coeff, sigma = next_sigma(sigma)
    for g in range(GROUPS):
        product_e(g)
    first_tile = (row // 2) * PAIR + odd_row * FOUR
    for g in range(GROUPS):
        value = reduce_e(g, scale, coeff)
        degrees = jnp.stack([pick_tiles[g * TPB + lax.rem(first_tile + t, TPB)] for t in range(FIVE)])
        spread_e(g, jnp.where(degrees == 0, kept_ref[g], value))

    for g in range(GROUPS):
        arrived(g, odd_row, gather_e, peers_e)
        for b in range(blocks_e):
            filtered_ref[g * GV:(g + 1) * GV, b * LANES:(b + 1) * LANES] = vec_e[
                g, b * TPB:(b + 1) * TPB].reshape(GV, LANES)
    for g in range(GROUPS):
        left(g, odd_row, gather_e, all_e)

    lane = lax.broadcasted_iota(jnp.int32, (NEV, LANES), 1)
    sublane = lax.broadcasted_iota(jnp.int32, (NEV, LANES), 0)

    def inverse_factor(buffer, send, recv):
        high, low = split_planes(filtered_ref[...])
        planes[0:NEV] = high
        planes[NEV:2 * NEV] = low
        gram = lax.dot_general(planes[...], planes[...], NT, preferred_element_type=F32)
        gram = gram[:NEV] + gram[NEV:]
        buffer[col, :, 0:NEV] = gram[:, :NEV] + gram[:, NEV:]
        for slot in all_o:
            gram_copy(buffer, send, recv, slot).start()
        for slot in all_o:
            gram_copy(buffer, send, recv, slot).wait()
        total = buffer[0]
        for i in range(1, 8):
            total = total + buffer[i]
        work[...] = jnp.where(lane < NEV, total, jnp.where(lane - NEV == sublane, 1.0, 0.0))

        def eliminate(i, carry):
            j = 2 * i
            rest = work[...]
            row_a, row_b = work[pl.ds(j, 1), :], work[pl.ds(j + 1, 1), :]
            at_a, at_b = lane == j, lane == j + 1

            def entry(mask, values):
                return jnp.sum(jnp.where(mask, values, 0.0), axis=1, keepdims=True)

            pivot_a = entry(at_a[0:1], row_a)
            cross = entry(at_b[0:1], row_a) / pivot_a
            pivot_b = entry(at_b[0:1], row_b) - cross * entry(at_b[0:1], row_a)
            column_a, column_b = entry(at_a, rest), entry(at_b, rest)
            row_b = row_b - cross * row_a
            below = sublane[:, 0:1] > j + 1
            factor_a = jnp.where(below, column_a / pivot_a, 0.0)
            factor_b = jnp.where(below, (column_b - cross * column_a) / pivot_b, 0.0)
            updated = rest - factor_a * row_a - factor_b * row_b
            work[...] = jnp.where(sublane == j, row_a * lax.rsqrt(pivot_a), jnp.where(
                sublane == j + 1, row_b * lax.rsqrt(pivot_b), updated))
            return carry

        lax.fori_loop(0, NEV // 2, eliminate, 0)
        return work[:, NEV:2 * NEV]

    first = jnp.dot(inverse_factor(gram_a, g_s, g_r), filtered_ref[...],
                    precision=lax.Precision.HIGHEST, preferred_element_type=F32)
    filtered_ref[...] = first
    order = jnp.sqrt(jnp.full((NEV, NEV), 8 * cols_dev, F32))
    out_ref[...] = jnp.dot(order * inverse_factor(gram_b, h_s, h_r), filtered_ref[...],
                           precision=lax.Precision.HIGHEST, preferred_element_type=F32)


def on_device(hamilton, start_block, bounds, degree_pick):
    rows_dev, cols_dev = hamilton.shape
    tiles_o = rows_dev // LANES * TPB
    tiles_e = cols_dev // LANES * TPB
    vmem = pltpu.VMEM
    dma = pltpu.SemaphoreType.DMA
    return pl.pallas_call(
        functools.partial(kernel, (rows_dev, cols_dev)),
        out_shape=jax.ShapeDtypeStruct((NEV, cols_dev), F32),
        in_specs=[
            pl.BlockSpec(memory_space=pl.ANY),
            pl.BlockSpec(memory_space=pltpu.VMEM),
            pl.BlockSpec(memory_space=pltpu.SMEM),
            pl.BlockSpec(memory_space=pltpu.SMEM),
        ],
        out_specs=pl.BlockSpec(memory_space=pltpu.VMEM),
        scratch_shapes=[
            vmem((SLOTS, CHUNK, cols_dev), F32),
            vmem((rows_dev, cols_dev), BF16),
            vmem((rows_dev, cols_dev), BF16),
            vmem((cols_dev, rows_dev), BF16),
            vmem((cols_dev, rows_dev), BF16),
            vmem((2 * NEV, cols_dev), BF16),
            vmem((2 * PADV, cols_dev), BF16),
            vmem((NEV, cols_dev), F32),
            vmem((GROUPS, tiles_o, SUB, LANES), F32),
            vmem((GROUPS, tiles_e, SUB, LANES), F32),
            vmem((GROUPS, 7, FIVE, SUB, LANES), F32),
            vmem((GROUPS, 15, FIVE, SUB, LANES), F32),
            vmem((GROUPS, tiles_o, SUB, LANES), F32),
            vmem((GROUPS, tiles_e, SUB, LANES), F32),
            vmem((GROUPS, FIVE, SUB, LANES), F32),
            vmem((GROUPS, FIVE, SUB, LANES), F32),
            vmem((GROUPS, FIVE, SUB, LANES), F32),
            vmem((NEV // SUB, SUB, LANES), jnp.int32),
            vmem((8, NEV, LANES), F32),
            vmem((8, NEV, LANES), F32),
            vmem((NEV, LANES), F32),
            dma((SLOTS,)),
            dma((GROUPS, 7)), dma((GROUPS, 7)), dma((GROUPS, 7)), dma((GROUPS, 7)),
            dma((GROUPS, 15)), dma((GROUPS, 15)), dma((GROUPS, 15)), dma((GROUPS, 15)),
            dma((GROUPS, 7)), dma((GROUPS, 7)), dma((GROUPS, 15)), dma((GROUPS, 15)),
            dma((7,)), dma((7,)), dma((7,)), dma((7,)),
        ],
        compiler_params=pltpu.CompilerParams(
            collective_id=0, has_side_effects=True, vmem_limit_bytes=62 * 2**20),
        cost_estimate=pl.CostEstimate(
            flops=2 * DHI * 4 * NEV * rows_dev * cols_dev,
            bytes_accessed=4 * rows_dev * cols_dev, transcendentals=0),
    )(hamilton, start_block, bounds, degree_pick)


def solution(mesh):
    in_specs = (P("row", "col"), P(None, "col"), P(), P())
    out_specs = P(None, "col")
    return jax.shard_map(
        on_device, mesh=mesh, in_specs=in_specs, out_specs=out_specs, check_vma=False
    )
```

```python
import functools

import jax
import jax.numpy as jnp
from jax import lax
from jax.experimental import pallas as pl
from jax.experimental.pallas import tpu as pltpu
from jax.sharding import PartitionSpec as P

DLO = 6
DHI = 10
NEV = 48
GROUPS = 2
GV = NEV // GROUPS
PADV = 32
LANES = 128
SUB = 8
TPB = GV // SUB
PAIR = 9
FIVE = 5
FOUR = 4
CHUNK = 256
SLOTS = 4
MESH = pl.DeviceIdType.MESH
NT = (((1,), (1,)), ((), ()))
NN = (((1,), (0,)), ((), ()))
FAR_FIRST = (2, 1, 3, 0)
F32 = jnp.float32
BF16 = jnp.bfloat16


def split_planes(value):
    high = value.astype(BF16)
    low = (value - high.astype(F32)).astype(BF16)
    return high, low


def kernel(
    sizes,
    ham_ref, start_hbm, bounds_ref, pick_ref, out_ref,
    stage, high_ref, low_ref, high_t, low_t, planes, group_planes, start_ref,
    part_o, part_e, land_o, land_e, vec_o, vec_e, last_o, last_e, kept_ref,
    pick_tiles, gram_a, gram_b, work,
    ham_sem, start_sem,
    rs_o_s, rs_o_r, ag_o_s, ag_o_r, rs_e_s, rs_e_r, ag_e_s, ag_e_r,
    g_s, g_r, h_s, h_r,
):
    rows_dev, cols_dev = sizes
    row = lax.axis_index("row")
    col = lax.axis_index("col")
    y, x = row // 4, lax.rem(row, 4)
    z, core = col // 2, lax.rem(col, 2)
    blocks_o, blocks_e = rows_dev // LANES, cols_dev // LANES
    wide = cols_dev // 4
    wide_tiles = wide // LANES * TPB
    odd_row = lax.rem(row, 2)

    peers_o = [(dz, dc) for dz in FAR_FIRST for dc in (0, 1) if (dz, dc) != (0, 0)]
    peers_e = [(dy, dx) for dy in FAR_FIRST for dx in FAR_FIRST if (dy, dx) != (0, 0)]
    all_o, all_e = range(len(peers_o)), range(len(peers_e))

    def index_o(offset):
        return lax.rem(z + offset[0], 4) * 2 + lax.rem(core + offset[1], 2)

    def index_e(offset):
        return lax.rem(y + offset[0], 4) * 4 + lax.rem(x + offset[1], 4)

    def shared(index, parity):
        if parity == 0:
            return pl.ds((index // 2) * PAIR, FIVE)
        return pl.ds((index // 2) * PAIR + FIVE, FOUR)

    def by_parity(odd, act):
        for parity in (0, 1):
            pl.when(odd == parity)(functools.partial(act, parity))

    def landing(land, g, slot, parity):
        return land.at[g, slot] if parity == 0 else land.at[g, slot, pl.ds(1, FOUR)]

    def remote(source, target, send, recv, device):
        return pltpu.make_async_remote_copy(
            src_ref=source, dst_ref=target, send_sem=send, recv_sem=recv,
            device_id=device, device_id_type=MESH)

    def scatter_o(g, slot, parity):
        to = index_o(peers_o[slot])
        return remote(part_o.at[g, shared(to, parity)], landing(land_o, g, slot, parity),
                      rs_o_s.at[g, slot], rs_o_r.at[g, slot], (row, to))

    def scatter_e(g, slot, parity):
        to = index_e(peers_e[slot])
        return remote(part_e.at[g, shared(to, parity)], landing(land_e, g, slot, parity),
                      rs_e_s.at[g, slot], rs_e_r.at[g, slot], (to, col))

    def gather_o(g, slot, parity):
        mine = vec_o.at[g, shared(col, parity)]
        return remote(mine, mine, ag_o_s.at[g, slot], ag_o_r.at[g, slot], (row, index_o(peers_o[slot])))

    def gather_e(g, slot, parity):
        mine = vec_e.at[g, shared(row, parity)]
        return remote(mine, mine, ag_e_s.at[g, slot], ag_e_r.at[g, slot], (index_e(peers_e[slot]), col))

    def partner(parity, offset):
        return (parity + offset[1]) % 2

    def spread(vec, g, value, index, odd, gather, slots):
        def act(parity):
            vec[g, shared(index, parity)] = value[parity:]
            for slot in slots:
                gather(g, slot, parity).start()

        by_parity(odd, act)

    def arrived(g, odd, gather, peers):
        def act(parity):
            for slot, offset in enumerate(peers):
                gather(g, slot, partner(parity, offset)).wait_recv()

        by_parity(odd, act)

    def left(g, odd, gather, slots):
        def act(parity):
            for slot in slots:
                gather(g, slot, parity).wait_send()

        by_parity(odd, act)

    def send_parts(g, odd, scatter, peers, slots):
        def act(parity):
            for slot in slots:
                scatter(g, slot, partner(parity, peers[slot])).start()

        by_parity(odd, act)

    def sent_parts(g, odd, scatter, peers):
        def act(parity):
            for slot, offset in enumerate(peers):
                scatter(g, slot, partner(parity, offset)).wait_send()

        by_parity(odd, act)

    def parts_here(g, odd, scatter, slots):
        def act(parity):
            for slot in slots:
                scatter(g, slot, parity).wait_recv()

        by_parity(odd, act)

    def summed(index):
        return pl.ds((index // 2) * PAIR + lax.rem(index, 2) * FOUR, FIVE)

    def gram_copy(buffer, send, recv, slot):
        return pltpu.make_async_remote_copy(
            src_ref=buffer.at[col], dst_ref=buffer.at[col],
            send_sem=send.at[slot], recv_sem=recv.at[slot],
            device_id=(row, index_o(peers_o[slot])), device_id_type=MESH)

    chunks = rows_dev // CHUNK

    def ham_copy(place):
        return pltpu.make_async_copy(
            ham_ref.at[place * CHUNK:(place + 1) * CHUNK], stage.at[place % SLOTS], ham_sem.at[place % SLOTS])

    start_copy = pltpu.make_async_copy(start_hbm, start_ref, start_sem)
    start_copy.start()
    for place in range(SLOTS):
        ham_copy(place).start()

    for g in range(GROUPS):
        for slot in all_o:
            land_o[g, slot, 0] = jnp.zeros((SUB, LANES), F32)
        for slot in all_e:
            land_e[g, slot, 0] = jnp.zeros((SUB, LANES), F32)
    gram_a[...] = jnp.zeros_like(gram_a)
    gram_b[...] = jnp.zeros_like(gram_b)
    barrier = pltpu.get_barrier_semaphore()
    for offset in peers_o:
        pl.semaphore_signal(barrier, inc=1, device_id=(row, index_o(offset)), device_id_type=MESH)
    for offset in peers_e:
        pl.semaphore_signal(barrier, inc=1, device_id=(index_e(offset), col), device_id_type=MESH)

    lowest = jnp.full((SUB, LANES), bounds_ref[0], F32)
    lower_end = jnp.full((SUB, LANES), bounds_ref[1], F32)
    upper_end = jnp.full((SUB, LANES), bounds_ref[2], F32)
    half_width = (upper_end - lower_end) / 2.0
    center = (upper_end + lower_end) / 2.0
    sigma_one = half_width / (lowest - center)

    tile_shape = (NEV // SUB, SUB, LANES)
    vector_at = lax.broadcasted_iota(jnp.int32, tile_shape, 0) * SUB + lax.broadcasted_iota(
        jnp.int32, tile_shape, 1)
    picked = jnp.zeros(tile_shape, jnp.int32)
    for v in range(NEV):
        picked = jnp.where(vector_at == v, pick_ref[v], picked)
    pick_tiles[...] = picked

    start_copy.wait()
    for b in range(blocks_e):
        value = start_ref[:, b * LANES:(b + 1) * LANES]
        high, low = split_planes(value)
        planes[0:NEV, b * LANES:(b + 1) * LANES] = high
        planes[NEV:2 * NEV, b * LANES:(b + 1) * LANES] = low
        for g in range(GROUPS):
            vec_e[g, b * TPB:(b + 1) * TPB] = value[g * GV:(g + 1) * GV].reshape(TPB, SUB, LANES)
    for g in range(GROUPS):
        last_e[g] = vec_e[g, summed(row)]
    last_o[...] = jnp.zeros_like(last_o)

    offset = row * rows_dev - col * cols_dev
    inside = (offset >= 0) & (offset < cols_dev)
    diag_at = jnp.where(inside, offset, 0)
    diag_weight = jnp.where(inside, 1.0, 0.0).astype(F32)
    eye = (lax.broadcasted_iota(jnp.int32, (LANES, LANES), 0)
           == lax.broadcasted_iota(jnp.int32, (LANES, LANES), 1))
    shift = jnp.where(eye, center[0:1] * diag_weight, 0.0)

    def store_tiles(part, g, first_tile, total):
        for b in range(total.shape[1] // LANES):
            part[g, pl.ds(first_tile + b * TPB, TPB)] = total[:, b * LANES:(b + 1) * LANES].reshape(
                TPB, SUB, LANES)

    def split_chunk(place):
        slot, first_row = place % SLOTS, place * CHUNK
        ham_copy(place).wait()
        for b in range(CHUNK // LANES):
            at = pl.ds(pl.multiple_of(diag_at + first_row + b * LANES, LANES), LANES)
            rows_at = slice(b * LANES, (b + 1) * LANES)
            stage[slot, rows_at, at] = stage[slot, rows_at, at] - shift
        for i in range(0, CHUNK, 16):
            high, low = split_planes(stage[slot, i:i + 16, :])
            high_ref[first_row + i:first_row + i + 16, :] = high
            low_ref[first_row + i:first_row + i + 16, :] = low

    def multiply_chunk(place):
        rows_at = slice(place * CHUNK, (place + 1) * CHUNK)
        total = (lax.dot_general(planes[...], high_ref[rows_at, :], NT, preferred_element_type=F32)
                 + lax.dot_general(planes[...], low_ref[rows_at, :], NT, preferred_element_type=F32))
        total = total[:NEV] + total[NEV:]
        for g in range(GROUPS):
            store_tiles(part_o, g, place * CHUNK // LANES * TPB, total[g * GV:(g + 1) * GV])

    def in_half(offset, half):
        return lax.rem(z + offset[0], 4) // 2 == half

    def send_half(half):
        for g in range(GROUPS):
            for slot, offset in enumerate(peers_o):
                pl.when(in_half(offset, half))(
                    functools.partial(send_parts, g, core, scatter_o, peers_o, (slot,)))

    split_chunk(0)
    for place in range(chunks):
        if place + SLOTS < chunks:
            ham_copy(place + SLOTS).start()
        if place + 1 < chunks:
            split_chunk(place + 1)
        multiply_chunk(place)
        if place == chunks // 2 - 1:
            pl.semaphore_wait(barrier, len(peers_o) + len(peers_e))
            send_half(0)
    send_half(1)

    def transpose(piece):
        rows_at = slice(piece * (rows_dev // 4), (piece + 1) * (rows_dev // 4))
        for j in range(0, cols_dev, 512):
            high_t[j:j + 512, rows_at] = high_ref[rows_at, j:j + 512].T
            low_t[j:j + 512, rows_at] = low_ref[rows_at, j:j + 512].T

    def reduce(g, scale, coeff, part, land, last, index, odd, scatter, slots):
        parts_here(g, odd, scatter, slots)
        total = part[g, summed(index)]
        for slot in slots:
            total = total + land[g, slot]
        value = scale * total - coeff * last[g]
        last[g] = value
        return value

    def reduce_o(g, scale, coeff):
        value = reduce(g, scale, coeff, part_o, land_o, last_o, col, core, scatter_o, all_o)
        spread(vec_o, g, value, col, core, gather_o, all_o)
        sent_parts(g, core, scatter_o, peers_o)

    def reduce_e(g, scale, coeff):
        return reduce(g, scale, coeff, part_e, land_e, last_e, row, odd_row, scatter_e, all_e)

    def spread_e(g, value):
        spread(vec_e, g, value, row, odd_row, gather_e, all_e)
        sent_parts(g, odd_row, scatter_e, peers_e)

    def to_planes(vec, g, blocks):
        nothing = jnp.zeros((PADV - GV, LANES), F32)
        for b in range(blocks):
            value = vec[g, b * TPB:(b + 1) * TPB].reshape(GV, LANES)
            high, low = split_planes(jnp.concatenate([value, nothing], axis=0))
            group_planes[0:PADV, b * LANES:(b + 1) * LANES] = high
            group_planes[PADV:2 * PADV, b * LANES:(b + 1) * LANES] = low

    def product(depth, high, low, target):
        cols_at = pl.ds(pl.multiple_of(target * wide, LANES), wide)
        vectors = group_planes[:, 0:depth]
        total = (lax.dot_general(vectors, high[:, cols_at], NN, preferred_element_type=F32)
                 + lax.dot_general(vectors, low[:, cols_at], NN, preferred_element_type=F32))
        return total[:GV] + total[PADV:PADV + GV]

    def product_e(g):
        arrived(g, core, gather_o, peers_o)
        to_planes(vec_o, g, blocks_o)
        for dy in FAR_FIRST:
            target = lax.rem(y + dy, 4)
            store_tiles(part_e, g, target * wide_tiles, product(rows_dev, high_ref, low_ref, target))
            send_parts(g, odd_row, scatter_e, peers_e, [s for s in all_e if peers_e[s][0] == dy])
        left(g, core, gather_o, all_o)

    def product_o(g):
        arrived(g, odd_row, gather_e, peers_e)
        to_planes(vec_e, g, blocks_e)
        for other in (1, 0):
            target = lax.rem(z // 2 + other, 2)
            store_tiles(part_o, g, target * wide_tiles, product(cols_dev, high_t, low_t, target))
            for slot, offset in enumerate(peers_o):
                pl.when(in_half(offset, target))(
                    functools.partial(send_parts, g, core, scatter_o, peers_o, (slot,)))
        left(g, odd_row, gather_e, all_e)

    def next_sigma(sigma):
        new_sigma = 1.0 / (2.0 / sigma_one - sigma)
        return 2.0 * new_sigma / half_width, sigma * new_sigma, new_sigma

    transpose(0)
    transpose(1)
    for g in range(GROUPS):
        reduce_o(g, sigma_one / half_width, 0.0 * sigma_one)
    transpose(2)
    transpose(3)

    def two_steps(pair, sigma):
        scale, coeff, sigma = next_sigma(sigma)
        for g in range(GROUPS):
            product_e(g)
        for g in range(GROUPS):
            value = reduce_e(g, scale, coeff)
            kept_ref[g] = jnp.where(pair == DLO // 2 - 1, value, kept_ref[g])
            spread_e(g, value)
        scale, coeff, sigma = next_sigma(sigma)
        for g in range(GROUPS):
            product_o(g)
        for g in range(GROUPS):
            reduce_o(g, scale, coeff)
        return sigma

    kept_ref[...] = jnp.zeros_like(kept_ref)
    sigma = lax.fori_loop(0, DHI // 2 - 1, two_steps, sigma_one)
    scale, coeff, sigma = next_sigma(sigma)
    for g in range(GROUPS):
        product_e(g)
    first_tile = (row // 2) * PAIR + odd_row * FOUR
    for g in range(GROUPS):
        value = reduce_e(g, scale, coeff)
        degrees = jnp.stack([pick_tiles[g * TPB + lax.rem(first_tile + t, TPB)] for t in range(FIVE)])
        spread_e(g, jnp.where(degrees == 0, kept_ref[g], value))

    for g in range(GROUPS):
        arrived(g, odd_row, gather_e, peers_e)
        for b in range(blocks_e):
            cols_at = slice(b * LANES, (b + 1) * LANES)
            start_ref[g * GV:(g + 1) * GV, cols_at] = vec_e[g, b * TPB:(b + 1) * TPB].reshape(GV, LANES)
    for g in range(GROUPS):
        left(g, odd_row, gather_e, all_e)

    lane = lax.broadcasted_iota(jnp.int32, (NEV, LANES), 1)
    sublane = lax.broadcasted_iota(jnp.int32, (NEV, LANES), 0)

    high, low = split_planes(start_ref[...])
    planes[0:NEV] = high
    planes[NEV:2 * NEV] = low

    def inverse_factor(buffer, send, recv):
        gram = lax.dot_general(planes[...], planes[...], NT, preferred_element_type=F32)
        gram = gram[:NEV] + gram[NEV:]
        gram = gram[:, :NEV] + gram[:, NEV:]
        buffer[col, :, 0:NEV] = gram[:GV]
        buffer[col, :, LANES // 2:LANES // 2 + NEV] = gram[GV:]
        for slot in all_o:
            gram_copy(buffer, send, recv, slot).start()
        for slot in all_o:
            gram_copy(buffer, send, recv, slot).wait()
        total = buffer[0]
        for i in range(1, 8):
            total = total + buffer[i]
        total = jnp.concatenate([total, pltpu.roll(total, LANES // 2, 1)], axis=0)
        work[...] = jnp.where(lane < NEV, total, jnp.where(lane - NEV == sublane, 1.0, 0.0))

        def eliminate(i, carry):
            j = 2 * i
            rest = work[...]
            row_a, row_b = work[pl.ds(j, 1), :], work[pl.ds(j + 1, 1), :]
            at_a, at_b = lane == j, lane == j + 1

            def entry(mask, values):
                return jnp.sum(jnp.where(mask, values, 0.0), axis=1, keepdims=True)

            pivot_a = entry(at_a[0:1], row_a)
            cross = entry(at_b[0:1], row_a) / pivot_a
            pivot_b = entry(at_b[0:1], row_b) - cross * entry(at_b[0:1], row_a)
            column_a, column_b = entry(at_a, rest), entry(at_b, rest)
            row_b = row_b - cross * row_a
            below = sublane[:, 0:1] > j + 1
            factor_a = jnp.where(below, column_a / pivot_a, 0.0)
            factor_b = jnp.where(below, (column_b - cross * column_a) / pivot_b, 0.0)
            updated = rest - factor_a * row_a - factor_b * row_b
            work[...] = jnp.where(sublane == j, row_a * lax.rsqrt(pivot_a), jnp.where(
                sublane == j + 1, row_b * lax.rsqrt(pivot_b), updated))
            return carry

        lax.fori_loop(0, NEV // 2, eliminate, 0)
        return work[:, NEV:2 * NEV]

    def apply_factor(factor, cols_at):
        high, low = split_planes(factor)
        factor_planes = jnp.concatenate([high, low], axis=0)
        total = (jnp.dot(factor_planes, planes[0:NEV, cols_at], preferred_element_type=F32)
                 + jnp.dot(factor_planes, planes[NEV:2 * NEV, cols_at], preferred_element_type=F32))
        return total[:NEV] + total[NEV:]

    factor = inverse_factor(gram_a, g_s, g_r)
    for j in range(0, cols_dev, wide):
        high, low = split_planes(apply_factor(factor, slice(j, j + wide)))
        planes[0:NEV, j:j + wide] = high
        planes[NEV:2 * NEV, j:j + wide] = low
    factor = jnp.sqrt(jnp.full((NEV, NEV), 8 * cols_dev, F32)) * inverse_factor(gram_b, h_s, h_r)
    for j in range(0, cols_dev, wide):
        out_ref[:, j:j + wide] = apply_factor(factor, slice(j, j + wide))


def on_device(hamilton, start_block, bounds, degree_pick):
    rows_dev, cols_dev = hamilton.shape
    tiles_o = rows_dev // LANES * TPB
    tiles_e = cols_dev // LANES * TPB
    vmem = pltpu.VMEM
    dma = pltpu.SemaphoreType.DMA
    return pl.pallas_call(
        functools.partial(kernel, (rows_dev, cols_dev)),
        out_shape=jax.ShapeDtypeStruct((NEV, cols_dev), F32),
        in_specs=[
            pl.BlockSpec(memory_space=pl.ANY),
            pl.BlockSpec(memory_space=pl.ANY),
            pl.BlockSpec(memory_space=pltpu.SMEM),
            pl.BlockSpec(memory_space=pltpu.SMEM),
        ],
        out_specs=pl.BlockSpec(memory_space=pltpu.VMEM),
        scratch_shapes=[
            vmem((SLOTS, CHUNK, cols_dev), F32),
            vmem((rows_dev, cols_dev), BF16),
            vmem((rows_dev, cols_dev), BF16),
            vmem((cols_dev, rows_dev), BF16),
            vmem((cols_dev, rows_dev), BF16),
            vmem((2 * NEV, cols_dev), BF16),
            vmem((2 * PADV, cols_dev), BF16),
            vmem((NEV, cols_dev), F32),
            vmem((GROUPS, tiles_o, SUB, LANES), F32),
            vmem((GROUPS, tiles_e, SUB, LANES), F32),
            vmem((GROUPS, 7, FIVE, SUB, LANES), F32),
            vmem((GROUPS, 15, FIVE, SUB, LANES), F32),
            vmem((GROUPS, tiles_o, SUB, LANES), F32),
            vmem((GROUPS, tiles_e, SUB, LANES), F32),
            vmem((GROUPS, FIVE, SUB, LANES), F32),
            vmem((GROUPS, FIVE, SUB, LANES), F32),
            vmem((GROUPS, FIVE, SUB, LANES), F32),
            vmem((NEV // SUB, SUB, LANES), jnp.int32),
            vmem((8, GV, LANES), F32),
            vmem((8, GV, LANES), F32),
            vmem((NEV, LANES), F32),
            dma((SLOTS,)),
            dma,
            dma((GROUPS, 7)), dma((GROUPS, 7)), dma((GROUPS, 7)), dma((GROUPS, 7)),
            dma((GROUPS, 15)), dma((GROUPS, 15)), dma((GROUPS, 15)), dma((GROUPS, 15)),
            dma((7,)), dma((7,)), dma((7,)), dma((7,)),
        ],
        compiler_params=pltpu.CompilerParams(
            collective_id=0, has_side_effects=True, vmem_limit_bytes=62 * 2**20),
        cost_estimate=pl.CostEstimate(
            flops=2 * DHI * 4 * NEV * rows_dev * cols_dev,
            bytes_accessed=4 * rows_dev * cols_dev, transcendentals=0),
    )(hamilton, start_block, bounds, degree_pick)


def solution(mesh):
    in_specs = (P("row", "col"), P(None, "col"), P(), P())
    out_specs = P(None, "col")
    return jax.shard_map(
        on_device, mesh=mesh, in_specs=in_specs, out_specs=out_specs, check_vma=False
    )
```

```python
import functools

import jax
import jax.numpy as jnp
from jax import lax
from jax.experimental import pallas as pl
from jax.experimental.pallas import tpu as pltpu
from jax.sharding import PartitionSpec as P

DLO = 6
DHI = 10
NEV = 48
GROUPS = 2
GV = NEV // GROUPS
PADV = 32
LANES = 128
SUB = 8
TPB = GV // SUB
PAIR = 9
FIVE = 5
FOUR = 4
CHUNK = 256
SLOTS = 4
MESH = pl.DeviceIdType.MESH
NT = (((1,), (1,)), ((), ()))
NN = (((1,), (0,)), ((), ()))
FAR_FIRST = (2, 1, 3, 0)
F32 = jnp.float32
BF16 = jnp.bfloat16


def split_planes(value):
    high = value.astype(BF16)
    low = (value - high.astype(F32)).astype(BF16)
    return high, low


def kernel(
    sizes,
    ham_ref, start_hbm, bounds_ref, pick_ref, out_ref,
    stage, high_ref, low_ref, high_t, low_t, planes, group_planes, start_ref,
    part_o, part_e, land_o, land_e, vec_o, vec_e, last_o, last_e, kept_ref,
    pick_tiles, gram_a, gram_b, work,
    ham_sem, start_sem,
    rs_o_s, rs_o_r, ag_o_s, ag_o_r, rs_e_s, rs_e_r, ag_e_s, ag_e_r,
    g_s, g_r, h_s, h_r,
):
    rows_dev, cols_dev = sizes
    row = lax.axis_index("row")
    col = lax.axis_index("col")
    y, x = row // 4, lax.rem(row, 4)
    z, core = col // 2, lax.rem(col, 2)
    blocks_o, blocks_e = rows_dev // LANES, cols_dev // LANES
    wide = cols_dev // 4
    wide_tiles = wide // LANES * TPB
    odd_row = lax.rem(row, 2)

    peers_o = [(dz, dc) for dz in FAR_FIRST for dc in (0, 1) if (dz, dc) != (0, 0)]
    peers_e = [(dy, dx) for dy in FAR_FIRST for dx in FAR_FIRST if (dy, dx) != (0, 0)]
    all_o, all_e = range(len(peers_o)), range(len(peers_e))

    def index_o(offset):
        return lax.rem(z + offset[0], 4) * 2 + lax.rem(core + offset[1], 2)

    def index_e(offset):
        return lax.rem(y + offset[0], 4) * 4 + lax.rem(x + offset[1], 4)

    def shared(index, parity):
        if parity == 0:
            return pl.ds((index // 2) * PAIR, FIVE)
        return pl.ds((index // 2) * PAIR + FIVE, FOUR)

    def by_parity(odd, act):
        for parity in (0, 1):
            pl.when(odd == parity)(functools.partial(act, parity))

    def landing(land, g, slot, parity):
        return land.at[g, slot] if parity == 0 else land.at[g, slot, pl.ds(1, FOUR)]

    def landing_all(land, g, parity):
        return land.at[g] if parity == 0 else land.at[g, :, pl.ds(1, FOUR)]

    def remote(source, target, send, recv, device):
        return pltpu.make_async_remote_copy(
            src_ref=source, dst_ref=target, send_sem=send, recv_sem=recv,
            device_id=device, device_id_type=MESH)

    def scatter_o(g, slot, parity):
        to = index_o(peers_o[slot])
        return remote(part_o.at[g, shared(to, parity)], landing(land_o, g, slot, parity),
                      rs_o_s.at[g], rs_o_r.at[g], (row, to))

    def scatter_e(g, slot, parity):
        to = index_e(peers_e[slot])
        return remote(part_e.at[g, shared(to, parity)], landing(land_e, g, slot, parity),
                      rs_e_s.at[g], rs_e_r.at[g], (to, col))

    def gather_o(g, slot, parity):
        mine = vec_o.at[g, shared(col, parity)]
        return remote(mine, mine, ag_o_s.at[g], ag_o_r.at[g], (row, index_o(peers_o[slot])))

    def gather_e(g, slot, parity):
        mine = vec_e.at[g, shared(row, parity)]
        return remote(mine, mine, ag_e_s.at[g], ag_e_r.at[g], (index_e(peers_e[slot]), col))

    def partner(parity, offset):
        return (parity + offset[1]) % 2

    def spread(vec, g, value, index, odd, gather, slots):
        def act(parity):
            vec[g, shared(index, parity)] = value[parity:]
            for slot in slots:
                gather(g, slot, parity).start()

        by_parity(odd, act)

    def everything(buffer, g, parity):
        return buffer.at[g, pl.ds(0, buffer.shape[1] - FIVE + parity)]

    def arrived(g, odd, vec, recv):
        def act(parity):
            whole = everything(vec, g, parity)
            remote(whole, whole, recv.at[g], recv.at[g], (row, index_o(peers_o[0]))).wait_recv()

        by_parity(odd, act)

    def left(g, odd, land, send):
        def act(parity):
            whole = landing_all(land, g, parity)
            remote(whole, whole, send.at[g], send.at[g], (row, index_o(peers_o[0]))).wait_send()

        by_parity(odd, act)

    def send_parts(g, odd, scatter, peers, slots):
        def act(parity):
            for slot in slots:
                scatter(g, slot, partner(parity, peers[slot])).start()

        by_parity(odd, act)

    def sent_parts(g, odd, part, send):
        def act(parity):
            whole = everything(part, g, parity)
            remote(whole, whole, send.at[g], send.at[g], (row, index_o(peers_o[0]))).wait_send()

        by_parity(odd, act)

    def parts_here(g, odd, land, recv):
        def act(parity):
            whole = landing_all(land, g, parity)
            remote(whole, whole, recv.at[g], recv.at[g], (row, index_o(peers_o[0]))).wait_recv()

        by_parity(odd, act)

    def summed(index):
        return pl.ds((index // 2) * PAIR + lax.rem(index, 2) * FOUR, FIVE)

    def gram_copy(buffer, send, recv, slot):
        return pltpu.make_async_remote_copy(
            src_ref=buffer.at[col], dst_ref=buffer.at[col],
            send_sem=send.at[slot], recv_sem=recv.at[slot],
            device_id=(row, index_o(peers_o[slot])), device_id_type=MESH)

    chunks = rows_dev // CHUNK

    def ham_copy(place):
        return pltpu.make_async_copy(
            ham_ref.at[place * CHUNK:(place + 1) * CHUNK], stage.at[place % SLOTS], ham_sem.at[place % SLOTS])

    start_copy = pltpu.make_async_copy(start_hbm, start_ref, start_sem)
    start_copy.start()
    for place in range(SLOTS):
        ham_copy(place).start()

    for g in range(GROUPS):
        for slot in all_o:
            land_o[g, slot, 0] = jnp.zeros((SUB, LANES), F32)
        for slot in all_e:
            land_e[g, slot, 0] = jnp.zeros((SUB, LANES), F32)
    gram_a[...] = jnp.zeros_like(gram_a)
    gram_b[...] = jnp.zeros_like(gram_b)
    barrier = pltpu.get_barrier_semaphore()
    for offset in peers_o:
        pl.semaphore_signal(barrier, inc=1, device_id=(row, index_o(offset)), device_id_type=MESH)
    for offset in peers_e:
        pl.semaphore_signal(barrier, inc=1, device_id=(index_e(offset), col), device_id_type=MESH)

    lowest = jnp.full((SUB, LANES), bounds_ref[0], F32)
    lower_end = jnp.full((SUB, LANES), bounds_ref[1], F32)
    upper_end = jnp.full((SUB, LANES), bounds_ref[2], F32)
    half_width = (upper_end - lower_end) / 2.0
    center = (upper_end + lower_end) / 2.0
    sigma_one = half_width / (lowest - center)

    tile_shape = (NEV // SUB, SUB, LANES)
    vector_at = lax.broadcasted_iota(jnp.int32, tile_shape, 0) * SUB + lax.broadcasted_iota(
        jnp.int32, tile_shape, 1)
    picked = jnp.zeros(tile_shape, jnp.int32)
    for v in range(NEV):
        picked = jnp.where(vector_at == v, pick_ref[v], picked)
    pick_tiles[...] = picked

    start_copy.wait()
    for b in range(blocks_e):
        value = start_ref[:, b * LANES:(b + 1) * LANES]
        high, low = split_planes(value)
        planes[0:NEV, b * LANES:(b + 1) * LANES] = high
        planes[NEV:2 * NEV, b * LANES:(b + 1) * LANES] = low
        for g in range(GROUPS):
            vec_e[g, b * TPB:(b + 1) * TPB] = value[g * GV:(g + 1) * GV].reshape(TPB, SUB, LANES)
    for g in range(GROUPS):
        last_e[g] = vec_e[g, summed(row)]
    last_o[...] = jnp.zeros_like(last_o)

    offset = row * rows_dev - col * cols_dev
    inside = (offset >= 0) & (offset < cols_dev)
    diag_at = jnp.where(inside, offset, 0)
    diag_weight = jnp.where(inside, 1.0, 0.0).astype(F32)
    eye = (lax.broadcasted_iota(jnp.int32, (LANES, LANES), 0)
           == lax.broadcasted_iota(jnp.int32, (LANES, LANES), 1))
    shift = jnp.where(eye, center[0:1] * diag_weight, 0.0)

    def store_tiles(part, g, first_tile, total):
        for b in range(total.shape[1] // LANES):
            part[g, pl.ds(first_tile + b * TPB, TPB)] = total[:, b * LANES:(b + 1) * LANES].reshape(
                TPB, SUB, LANES)

    def split_chunk(place):
        slot, first_row = place % SLOTS, place * CHUNK
        ham_copy(place).wait()
        for b in range(CHUNK // LANES):
            at = pl.ds(pl.multiple_of(diag_at + first_row + b * LANES, LANES), LANES)
            rows_at = slice(b * LANES, (b + 1) * LANES)
            stage[slot, rows_at, at] = stage[slot, rows_at, at] - shift
        for i in range(0, CHUNK, 16):
            high, low = split_planes(stage[slot, i:i + 16, :])
            high_ref[first_row + i:first_row + i + 16, :] = high
            low_ref[first_row + i:first_row + i + 16, :] = low

    def multiply_chunk(place):
        rows_at = slice(place * CHUNK, (place + 1) * CHUNK)
        total = (lax.dot_general(planes[...], high_ref[rows_at, :], NT, preferred_element_type=F32)
                 + lax.dot_general(planes[...], low_ref[rows_at, :], NT, preferred_element_type=F32))
        total = total[:NEV] + total[NEV:]
        for g in range(GROUPS):
            store_tiles(part_o, g, place * CHUNK // LANES * TPB, total[g * GV:(g + 1) * GV])

    def in_half(offset, half):
        return lax.rem(z + offset[0], 4) // 2 == half

    def send_half(half):
        for g in range(GROUPS):
            for slot, offset in enumerate(peers_o):
                pl.when(in_half(offset, half))(
                    functools.partial(send_parts, g, core, scatter_o, peers_o, (slot,)))

    split_chunk(0)
    for place in range(chunks):
        if place + SLOTS < chunks:
            ham_copy(place + SLOTS).start()
        if place + 1 < chunks:
            split_chunk(place + 1)
        multiply_chunk(place)
        if place == chunks // 2 - 1:
            pl.semaphore_wait(barrier, len(peers_o) + len(peers_e))
            send_half(0)
    send_half(1)

    def transpose(piece):
        rows_at = slice(piece * (rows_dev // 4), (piece + 1) * (rows_dev // 4))
        for j in range(0, cols_dev, 512):
            high_t[j:j + 512, rows_at] = high_ref[rows_at, j:j + 512].T
            low_t[j:j + 512, rows_at] = low_ref[rows_at, j:j + 512].T

    def reduce(g, scale, coeff, part, land, last, index, odd, recv, slots):
        parts_here(g, odd, land, recv)
        total = part[g, summed(index)]
        for slot in slots:
            total = total + land[g, slot]
        value = scale * total - coeff * last[g]
        last[g] = value
        return value

    def reduce_o(g, scale, coeff):
        value = reduce(g, scale, coeff, part_o, land_o, last_o, col, core, rs_o_r, all_o)
        spread(vec_o, g, value, col, core, gather_o, all_o)
        sent_parts(g, core, part_o, rs_o_s)

    def reduce_e(g, scale, coeff):
        return reduce(g, scale, coeff, part_e, land_e, last_e, row, odd_row, rs_e_r, all_e)

    def spread_e(g, value):
        spread(vec_e, g, value, row, odd_row, gather_e, all_e)
        sent_parts(g, odd_row, part_e, rs_e_s)

    def to_planes(vec, g, blocks):
        nothing = jnp.zeros((PADV - GV, LANES), F32)
        for b in range(blocks):
            value = vec[g, b * TPB:(b + 1) * TPB].reshape(GV, LANES)
            high, low = split_planes(jnp.concatenate([value, nothing], axis=0))
            group_planes[0:PADV, b * LANES:(b + 1) * LANES] = high
            group_planes[PADV:2 * PADV, b * LANES:(b + 1) * LANES] = low

    def product(depth, high, low, target):
        cols_at = pl.ds(pl.multiple_of(target * wide, LANES), wide)
        vectors = group_planes[:, 0:depth]
        total = (lax.dot_general(vectors, high[:, cols_at], NN, preferred_element_type=F32)
                 + lax.dot_general(vectors, low[:, cols_at], NN, preferred_element_type=F32))
        return total[:GV] + total[PADV:PADV + GV]

    def product_e(g):
        arrived(g, core, vec_o, ag_o_r)
        to_planes(vec_o, g, blocks_o)
        for dy in FAR_FIRST:
            target = lax.rem(y + dy, 4)
            store_tiles(part_e, g, target * wide_tiles, product(rows_dev, high_ref, low_ref, target))
            send_parts(g, odd_row, scatter_e, peers_e, [s for s in all_e if peers_e[s][0] == dy])
        left(g, core, land_o, ag_o_s)

    def product_o(g):
        arrived(g, odd_row, vec_e, ag_e_r)
        to_planes(vec_e, g, blocks_e)
        for other in (1, 0):
            target = lax.rem(z // 2 + other, 2)
            store_tiles(part_o, g, target * wide_tiles, product(cols_dev, high_t, low_t, target))
            for slot, offset in enumerate(peers_o):
                pl.when(in_half(offset, target))(
                    functools.partial(send_parts, g, core, scatter_o, peers_o, (slot,)))
        left(g, odd_row, land_e, ag_e_s)

    def next_sigma(sigma):
        new_sigma = 1.0 / (2.0 / sigma_one - sigma)
        return 2.0 * new_sigma / half_width, sigma * new_sigma, new_sigma

    transpose(0)
    transpose(1)
    for g in range(GROUPS):
        reduce_o(g, sigma_one / half_width, 0.0 * sigma_one)
    transpose(2)
    transpose(3)

    def two_steps(pair, sigma):
        scale, coeff, sigma = next_sigma(sigma)
        for g in range(GROUPS):
            product_e(g)
        for g in range(GROUPS):
            value = reduce_e(g, scale, coeff)
            kept_ref[g] = jnp.where(pair == DLO // 2 - 1, value, kept_ref[g])
            spread_e(g, value)
        scale, coeff, sigma = next_sigma(sigma)
        for g in range(GROUPS):
            product_o(g)
        for g in range(GROUPS):
            reduce_o(g, scale, coeff)
        return sigma

    kept_ref[...] = jnp.zeros_like(kept_ref)
    sigma = lax.fori_loop(0, DHI // 2 - 1, two_steps, sigma_one)
    scale, coeff, sigma = next_sigma(sigma)
    for g in range(GROUPS):
        product_e(g)
    first_tile = (row // 2) * PAIR + odd_row * FOUR
    for g in range(GROUPS):
        value = reduce_e(g, scale, coeff)
        degrees = jnp.stack([pick_tiles[g * TPB + lax.rem(first_tile + t, TPB)] for t in range(FIVE)])
        spread_e(g, jnp.where(degrees == 0, kept_ref[g], value))

    for g in range(GROUPS):
        arrived(g, odd_row, vec_e, ag_e_r)
        for b in range(blocks_e):
            cols_at = slice(b * LANES, (b + 1) * LANES)
            start_ref[g * GV:(g + 1) * GV, cols_at] = vec_e[g, b * TPB:(b + 1) * TPB].reshape(GV, LANES)
    for g in range(GROUPS):
        left(g, odd_row, land_e, ag_e_s)

    lane = lax.broadcasted_iota(jnp.int32, (NEV, LANES), 1)
    sublane = lax.broadcasted_iota(jnp.int32, (NEV, LANES), 0)

    high, low = split_planes(start_ref[...])
    planes[0:NEV] = high
    planes[NEV:2 * NEV] = low

    def inverse_factor(buffer, send, recv):
        gram = lax.dot_general(planes[...], planes[...], NT, preferred_element_type=F32)
        gram = gram[:NEV] + gram[NEV:]
        gram = gram[:, :NEV] + gram[:, NEV:]
        buffer[col, :, 0:NEV] = gram[:GV]
        buffer[col, :, LANES // 2:LANES // 2 + NEV] = gram[GV:]
        for slot in all_o:
            gram_copy(buffer, send, recv, slot).start()
        for slot in all_o:
            gram_copy(buffer, send, recv, slot).wait()
        total = buffer[0]
        for i in range(1, 8):
            total = total + buffer[i]
        total = jnp.concatenate([total, pltpu.roll(total, LANES // 2, 1)], axis=0)
        work[...] = jnp.where(lane < NEV, total, jnp.where(lane - NEV == sublane, 1.0, 0.0))

        def eliminate(i, carry):
            j = 2 * i
            rest = work[...]
            row_a, row_b = work[pl.ds(j, 1), :], work[pl.ds(j + 1, 1), :]
            at_a, at_b = lane == j, lane == j + 1

            def entry(mask, values):
                return jnp.sum(jnp.where(mask, values, 0.0), axis=1, keepdims=True)

            pivot_a = entry(at_a[0:1], row_a)
            cross = entry(at_b[0:1], row_a) / pivot_a
            pivot_b = entry(at_b[0:1], row_b) - cross * entry(at_b[0:1], row_a)
            column_a, column_b = entry(at_a, rest), entry(at_b, rest)
            row_b = row_b - cross * row_a
            below = sublane[:, 0:1] > j + 1
            factor_a = jnp.where(below, column_a / pivot_a, 0.0)
            factor_b = jnp.where(below, (column_b - cross * column_a) / pivot_b, 0.0)
            updated = rest - factor_a * row_a - factor_b * row_b
            work[...] = jnp.where(sublane == j, row_a * lax.rsqrt(pivot_a), jnp.where(
                sublane == j + 1, row_b * lax.rsqrt(pivot_b), updated))
            return carry

        lax.fori_loop(0, NEV // 2, eliminate, 0)
        return work[:, NEV:2 * NEV]

    def apply_factor(factor, cols_at):
        high, low = split_planes(factor)
        factor_planes = jnp.concatenate([high, low], axis=0)
        total = (jnp.dot(factor_planes, planes[0:NEV, cols_at], preferred_element_type=F32)
                 + jnp.dot(factor_planes, planes[NEV:2 * NEV, cols_at], preferred_element_type=F32))
        return total[:NEV] + total[NEV:]

    factor = inverse_factor(gram_a, g_s, g_r)
    for j in range(0, cols_dev, wide):
        high, low = split_planes(apply_factor(factor, slice(j, j + wide)))
        planes[0:NEV, j:j + wide] = high
        planes[NEV:2 * NEV, j:j + wide] = low
    factor = jnp.sqrt(jnp.full((NEV, NEV), 8 * cols_dev, F32)) * inverse_factor(gram_b, h_s, h_r)
    for j in range(0, cols_dev, wide):
        out_ref[:, j:j + wide] = apply_factor(factor, slice(j, j + wide))


def on_device(hamilton, start_block, bounds, degree_pick):
    rows_dev, cols_dev = hamilton.shape
    tiles_o = rows_dev // LANES * TPB
    tiles_e = cols_dev // LANES * TPB
    vmem = pltpu.VMEM
    dma = pltpu.SemaphoreType.DMA
    return pl.pallas_call(
        functools.partial(kernel, (rows_dev, cols_dev)),
        out_shape=jax.ShapeDtypeStruct((NEV, cols_dev), F32),
        in_specs=[
            pl.BlockSpec(memory_space=pl.ANY),
            pl.BlockSpec(memory_space=pl.ANY),
            pl.BlockSpec(memory_space=pltpu.SMEM),
            pl.BlockSpec(memory_space=pltpu.SMEM),
        ],
        out_specs=pl.BlockSpec(memory_space=pltpu.VMEM),
        scratch_shapes=[
            vmem((SLOTS, CHUNK, cols_dev), F32),
            vmem((rows_dev, cols_dev), BF16),
            vmem((rows_dev, cols_dev), BF16),
            vmem((cols_dev, rows_dev), BF16),
            vmem((cols_dev, rows_dev), BF16),
            vmem((2 * NEV, cols_dev), BF16),
            vmem((2 * PADV, cols_dev), BF16),
            vmem((NEV, cols_dev), F32),
            vmem((GROUPS, tiles_o, SUB, LANES), F32),
            vmem((GROUPS, tiles_e, SUB, LANES), F32),
            vmem((GROUPS, 7, FIVE, SUB, LANES), F32),
            vmem((GROUPS, 15, FIVE, SUB, LANES), F32),
            vmem((GROUPS, tiles_o, SUB, LANES), F32),
            vmem((GROUPS, tiles_e, SUB, LANES), F32),
            vmem((GROUPS, FIVE, SUB, LANES), F32),
            vmem((GROUPS, FIVE, SUB, LANES), F32),
            vmem((GROUPS, FIVE, SUB, LANES), F32),
            vmem((NEV // SUB, SUB, LANES), jnp.int32),
            vmem((8, GV, LANES), F32),
            vmem((8, GV, LANES), F32),
            vmem((NEV, LANES), F32),
            dma((SLOTS,)),
            dma,
            dma((GROUPS,)), dma((GROUPS,)), dma((GROUPS,)), dma((GROUPS,)),
            dma((GROUPS,)), dma((GROUPS,)), dma((GROUPS,)), dma((GROUPS,)),
            dma((7,)), dma((7,)), dma((7,)), dma((7,)),
        ],
        compiler_params=pltpu.CompilerParams(
            collective_id=0, has_side_effects=True, vmem_limit_bytes=62 * 2**20),
        cost_estimate=pl.CostEstimate(
            flops=2 * DHI * 4 * NEV * rows_dev * cols_dev,
            bytes_accessed=4 * rows_dev * cols_dev, transcendentals=0),
    )(hamilton, start_block, bounds, degree_pick)


def solution(mesh):
    in_specs = (P("row", "col"), P(None, "col"), P(), P())
    out_specs = P(None, "col")
    return jax.shard_map(
        on_device, mesh=mesh, in_specs=in_specs, out_specs=out_specs, check_vma=False
    )
```

```python
import functools

import jax
import jax.numpy as jnp
from jax import lax
from jax.experimental import pallas as pl
from jax.experimental.pallas import tpu as pltpu
from jax.sharding import PartitionSpec as P

DLO = 6
DHI = 10
NEV = 48
GROUPS = 2
GV = NEV // GROUPS
PADV = 32
LANES = 128
SUB = 8
TPB = GV // SUB
PAIR = 9
FIVE = 5
FOUR = 4
CHUNK = 256
SLOTS = 4
MESH = pl.DeviceIdType.MESH
NT = (((1,), (1,)), ((), ()))
NN = (((1,), (0,)), ((), ()))
FAR_FIRST = (2, 1, 3, 0)
F32 = jnp.float32
BF16 = jnp.bfloat16


def split_planes(value):
    high = value.astype(BF16)
    low = (value - high.astype(F32)).astype(BF16)
    return high, low


def kernel(
    sizes,
    ham_ref, start_hbm, bounds_ref, pick_ref, out_ref,
    stage, high_ref, low_ref, high_t, low_t, planes, group_planes, start_ref,
    part_o, part_e, land_o, land_e, vec_o, vec_e, last_o, last_e, kept_ref,
    pick_tiles, gram_a, gram_b, work,
    ham_sem, start_sem,
    rs_o_s, rs_o_r, ag_o_s, ag_o_r, rs_e_s, rs_e_r, ag_e_s, ag_e_r,
    g_s, g_r, h_s, h_r,
):
    rows_dev, cols_dev = sizes
    row = lax.axis_index("row")
    col = lax.axis_index("col")
    y, x = row // 4, lax.rem(row, 4)
    z, core = col // 2, lax.rem(col, 2)
    blocks_o, blocks_e = rows_dev // LANES, cols_dev // LANES
    wide = cols_dev // 4
    wide_tiles = wide // LANES * TPB
    odd_row = lax.rem(row, 2)

    peers_o = [(dz, dc) for dz in FAR_FIRST for dc in (0, 1) if (dz, dc) != (0, 0)]
    peers_e = [(dy, dx) for dy in FAR_FIRST for dx in FAR_FIRST if (dy, dx) != (0, 0)]
    all_o, all_e = range(len(peers_o)), range(len(peers_e))

    def index_o(offset):
        return lax.rem(z + offset[0], 4) * 2 + lax.rem(core + offset[1], 2)

    def index_e(offset):
        return lax.rem(y + offset[0], 4) * 4 + lax.rem(x + offset[1], 4)

    def shared(index, parity):
        if parity == 0:
            return pl.ds((index // 2) * PAIR, FIVE)
        return pl.ds((index // 2) * PAIR + FIVE, FOUR)

    def by_parity(odd, act):
        for parity in (0, 1):
            pl.when(odd == parity)(functools.partial(act, parity))

    def landing(land, g, slot, parity):
        return land.at[g, slot] if parity == 0 else land.at[g, slot, pl.ds(1, FOUR)]

    def landing_all(land, g, parity):
        return land.at[g] if parity == 0 else land.at[g, :, pl.ds(1, FOUR)]

    def remote(source, target, send, recv, device):
        return pltpu.make_async_remote_copy(
            src_ref=source, dst_ref=target, send_sem=send, recv_sem=recv,
            device_id=device, device_id_type=MESH)

    def scatter_o(g, slot, parity):
        to = index_o(peers_o[slot])
        return remote(part_o.at[g, shared(to, parity)], landing(land_o, g, slot, parity),
                      rs_o_s.at[g], rs_o_r.at[g], (row, to))

    def scatter_e(g, slot, parity):
        to = index_e(peers_e[slot])
        return remote(part_e.at[g, shared(to, parity)], landing(land_e, g, slot, parity),
                      rs_e_s.at[g], rs_e_r.at[g], (to, col))

    def gather_o(g, slot, parity):
        mine = vec_o.at[g, shared(col, parity)]
        return remote(mine, mine, ag_o_s.at[g], ag_o_r.at[g], (row, index_o(peers_o[slot])))

    def gather_e(g, slot, parity):
        mine = vec_e.at[g, shared(row, parity)]
        return remote(mine, mine, ag_e_s.at[g], ag_e_r.at[g], (index_e(peers_e[slot]), col))

    def partner(parity, offset):
        return (parity + offset[1]) % 2

    def spread(vec, g, value, index, odd, gather, slots):
        def act(parity):
            vec[g, shared(index, parity)] = value[parity:]
            for slot in slots:
                gather(g, slot, parity).start()

        by_parity(odd, act)

    def everything(buffer, g, parity):
        return buffer.at[g, pl.ds(0, buffer.shape[1] - FIVE + parity)]

    def arrived(g, odd, vec, recv):
        def act(parity):
            whole = everything(vec, g, parity)
            remote(whole, whole, recv.at[g], recv.at[g], (row, index_o(peers_o[0]))).wait_recv()

        by_parity(odd, act)

    def left(g, odd, land, send):
        def act(parity):
            whole = landing_all(land, g, parity)
            remote(whole, whole, send.at[g], send.at[g], (row, index_o(peers_o[0]))).wait_send()

        by_parity(odd, act)

    def send_parts(g, odd, scatter, peers, slots):
        def act(parity):
            for slot in slots:
                scatter(g, slot, partner(parity, peers[slot])).start()

        by_parity(odd, act)

    def sent_parts(g, odd, part, send):
        def act(parity):
            whole = everything(part, g, parity)
            remote(whole, whole, send.at[g], send.at[g], (row, index_o(peers_o[0]))).wait_send()

        by_parity(odd, act)

    def parts_here(g, odd, land, recv):
        def act(parity):
            whole = landing_all(land, g, parity)
            remote(whole, whole, recv.at[g], recv.at[g], (row, index_o(peers_o[0]))).wait_recv()

        by_parity(odd, act)

    def summed(index):
        return pl.ds((index // 2) * PAIR + lax.rem(index, 2) * FOUR, FIVE)

    def gram_copy(buffer, send, recv, slot):
        return pltpu.make_async_remote_copy(
            src_ref=buffer.at[col], dst_ref=buffer.at[col],
            send_sem=send, recv_sem=recv,
            device_id=(row, index_o(peers_o[slot])), device_id_type=MESH)

    chunks = rows_dev // CHUNK

    def ham_copy(place):
        return pltpu.make_async_copy(
            ham_ref.at[place * CHUNK:(place + 1) * CHUNK], stage.at[place % SLOTS], ham_sem.at[place % SLOTS])

    start_copy = pltpu.make_async_copy(start_hbm, start_ref, start_sem)
    start_copy.start()
    for place in range(SLOTS):
        ham_copy(place).start()

    for g in range(GROUPS):
        for slot in all_o:
            land_o[g, slot, 0] = jnp.zeros((SUB, LANES), F32)
        for slot in all_e:
            land_e[g, slot, 0] = jnp.zeros((SUB, LANES), F32)
    gram_a[...] = jnp.zeros_like(gram_a)
    gram_b[...] = jnp.zeros_like(gram_b)
    barrier = pltpu.get_barrier_semaphore()
    for offset in peers_o:
        pl.semaphore_signal(barrier, inc=1, device_id=(row, index_o(offset)), device_id_type=MESH)
    for offset in peers_e:
        pl.semaphore_signal(barrier, inc=1, device_id=(index_e(offset), col), device_id_type=MESH)

    lowest = jnp.full((SUB, LANES), bounds_ref[0], F32)
    lower_end = jnp.full((SUB, LANES), bounds_ref[1], F32)
    upper_end = jnp.full((SUB, LANES), bounds_ref[2], F32)
    half_width = (upper_end - lower_end) / 2.0
    center = (upper_end + lower_end) / 2.0
    sigma_one = half_width / (lowest - center)

    tile_shape = (NEV // SUB, SUB, LANES)
    vector_at = lax.broadcasted_iota(jnp.int32, tile_shape, 0) * SUB + lax.broadcasted_iota(
        jnp.int32, tile_shape, 1)
    picked = jnp.zeros(tile_shape, jnp.int32)
    for v in range(NEV):
        picked = jnp.where(vector_at == v, pick_ref[v], picked)
    pick_tiles[...] = picked

    start_copy.wait()
    for b in range(blocks_e):
        value = start_ref[:, b * LANES:(b + 1) * LANES]
        high, low = split_planes(value)
        planes[0:NEV, b * LANES:(b + 1) * LANES] = high
        planes[NEV:2 * NEV, b * LANES:(b + 1) * LANES] = low
        for g in range(GROUPS):
            vec_e[g, b * TPB:(b + 1) * TPB] = value[g * GV:(g + 1) * GV].reshape(TPB, SUB, LANES)
    for g in range(GROUPS):
        last_e[g] = vec_e[g, summed(row)]
    last_o[...] = jnp.zeros_like(last_o)

    offset = row * rows_dev - col * cols_dev
    inside = (offset >= 0) & (offset < cols_dev)
    diag_at = jnp.where(inside, offset, 0)
    diag_weight = jnp.where(inside, 1.0, 0.0).astype(F32)
    eye = (lax.broadcasted_iota(jnp.int32, (LANES, LANES), 0)
           == lax.broadcasted_iota(jnp.int32, (LANES, LANES), 1))
    shift = jnp.where(eye, center[0:1] * diag_weight, 0.0)

    def store_tiles(part, g, first_tile, total):
        for b in range(total.shape[1] // LANES):
            part[g, pl.ds(first_tile + b * TPB, TPB)] = total[:, b * LANES:(b + 1) * LANES].reshape(
                TPB, SUB, LANES)

    def split_chunk(place):
        slot, first_row = place % SLOTS, place * CHUNK
        ham_copy(place).wait()
        for b in range(CHUNK // LANES):
            at = pl.ds(pl.multiple_of(diag_at + first_row + b * LANES, LANES), LANES)
            rows_at = slice(b * LANES, (b + 1) * LANES)
            stage[slot, rows_at, at] = stage[slot, rows_at, at] - shift
        for i in range(0, CHUNK, 16):
            high, low = split_planes(stage[slot, i:i + 16, :])
            high_ref[first_row + i:first_row + i + 16, :] = high
            low_ref[first_row + i:first_row + i + 16, :] = low

    def multiply_chunk(place):
        rows_at = slice(place * CHUNK, (place + 1) * CHUNK)
        total = (lax.dot_general(planes[...], high_ref[rows_at, :], NT, preferred_element_type=F32)
                 + lax.dot_general(planes[...], low_ref[rows_at, :], NT, preferred_element_type=F32))
        total = total[:NEV] + total[NEV:]
        for g in range(GROUPS):
            store_tiles(part_o, g, place * CHUNK // LANES * TPB, total[g * GV:(g + 1) * GV])

    def in_half(offset, half):
        return lax.rem(z + offset[0], 4) // 2 == half

    def send_half(half):
        for g in range(GROUPS):
            for slot, offset in enumerate(peers_o):
                pl.when(in_half(offset, half))(
                    functools.partial(send_parts, g, core, scatter_o, peers_o, (slot,)))

    split_chunk(0)
    for place in range(chunks):
        if place + SLOTS < chunks:
            ham_copy(place + SLOTS).start()
        if place + 1 < chunks:
            split_chunk(place + 1)
        multiply_chunk(place)
        if place == chunks // 2 - 1:
            pl.semaphore_wait(barrier, len(peers_o) + len(peers_e))
            send_half(0)
    send_half(1)

    def transpose(piece):
        rows_at = slice(piece * (rows_dev // 4), (piece + 1) * (rows_dev // 4))
        for j in range(0, cols_dev, 512):
            high_t[j:j + 512, rows_at] = high_ref[rows_at, j:j + 512].T
            low_t[j:j + 512, rows_at] = low_ref[rows_at, j:j + 512].T

    def reduce(g, scale, coeff, part, land, last, index, odd, recv, slots):
        parts_here(g, odd, land, recv)
        total = part[g, summed(index)]
        for slot in slots:
            total = total + land[g, slot]
        value = scale * total - coeff * last[g]
        last[g] = value
        return value

    def reduce_o(g, scale, coeff):
        value = reduce(g, scale, coeff, part_o, land_o, last_o, col, core, rs_o_r, all_o)
        spread(vec_o, g, value, col, core, gather_o, all_o)
        sent_parts(g, core, part_o, rs_o_s)

    def reduce_e(g, scale, coeff):
        return reduce(g, scale, coeff, part_e, land_e, last_e, row, odd_row, rs_e_r, all_e)

    def spread_e(g, value):
        spread(vec_e, g, value, row, odd_row, gather_e, all_e)
        sent_parts(g, odd_row, part_e, rs_e_s)

    def to_planes(vec, g, blocks):
        nothing = jnp.zeros((PADV - GV, LANES), F32)
        for b in range(blocks):
            value = vec[g, b * TPB:(b + 1) * TPB].reshape(GV, LANES)
            high, low = split_planes(jnp.concatenate([value, nothing], axis=0))
            group_planes[0:PADV, b * LANES:(b + 1) * LANES] = high
            group_planes[PADV:2 * PADV, b * LANES:(b + 1) * LANES] = low

    def product(depth, high, low, target):
        cols_at = pl.ds(pl.multiple_of(target * wide, LANES), wide)
        vectors = group_planes[:, 0:depth]
        total = (lax.dot_general(vectors, high[:, cols_at], NN, preferred_element_type=F32)
                 + lax.dot_general(vectors, low[:, cols_at], NN, preferred_element_type=F32))
        return total[:GV] + total[PADV:PADV + GV]

    def product_e(g):
        arrived(g, core, vec_o, ag_o_r)
        to_planes(vec_o, g, blocks_o)
        for dy in FAR_FIRST:
            target = lax.rem(y + dy, 4)
            store_tiles(part_e, g, target * wide_tiles, product(rows_dev, high_ref, low_ref, target))
            send_parts(g, odd_row, scatter_e, peers_e, [s for s in all_e if peers_e[s][0] == dy])
        left(g, core, land_o, ag_o_s)

    def product_o(g):
        arrived(g, odd_row, vec_e, ag_e_r)
        to_planes(vec_e, g, blocks_e)
        for other in (1, 0):
            target = lax.rem(z // 2 + other, 2)
            store_tiles(part_o, g, target * wide_tiles, product(cols_dev, high_t, low_t, target))
            for slot, offset in enumerate(peers_o):
                pl.when(in_half(offset, target))(
                    functools.partial(send_parts, g, core, scatter_o, peers_o, (slot,)))
        left(g, odd_row, land_e, ag_e_s)

    def next_sigma(sigma):
        new_sigma = 1.0 / (2.0 / sigma_one - sigma)
        return 2.0 * new_sigma / half_width, sigma * new_sigma, new_sigma

    transpose(0)
    transpose(1)
    for g in range(GROUPS):
        reduce_o(g, sigma_one / half_width, 0.0 * sigma_one)
    transpose(2)
    transpose(3)

    def two_steps(pair, sigma):
        scale, coeff, sigma = next_sigma(sigma)
        for g in range(GROUPS):
            product_e(g)
        for g in range(GROUPS):
            value = reduce_e(g, scale, coeff)
            kept_ref[g] = jnp.where(pair == DLO // 2 - 1, value, kept_ref[g])
            spread_e(g, value)
        scale, coeff, sigma = next_sigma(sigma)
        for g in range(GROUPS):
            product_o(g)
        for g in range(GROUPS):
            reduce_o(g, scale, coeff)
        return sigma

    kept_ref[...] = jnp.zeros_like(kept_ref)
    sigma = lax.fori_loop(0, DHI // 2 - 1, two_steps, sigma_one)
    scale, coeff, sigma = next_sigma(sigma)
    for g in range(GROUPS):
        product_e(g)
    first_tile = (row // 2) * PAIR + odd_row * FOUR
    for g in range(GROUPS):
        value = reduce_e(g, scale, coeff)
        degrees = jnp.stack([pick_tiles[g * TPB + lax.rem(first_tile + t, TPB)] for t in range(FIVE)])
        spread_e(g, jnp.where(degrees == 0, kept_ref[g], value))

    for g in range(GROUPS):
        arrived(g, odd_row, vec_e, ag_e_r)
        for b in range(blocks_e):
            cols_at = slice(b * LANES, (b + 1) * LANES)
            start_ref[g * GV:(g + 1) * GV, cols_at] = vec_e[g, b * TPB:(b + 1) * TPB].reshape(GV, LANES)
    for g in range(GROUPS):
        left(g, odd_row, land_e, ag_e_s)

    lane = lax.broadcasted_iota(jnp.int32, (NEV, LANES), 1)
    sublane = lax.broadcasted_iota(jnp.int32, (NEV, LANES), 0)

    high, low = split_planes(start_ref[...])
    planes[0:NEV] = high
    planes[NEV:2 * NEV] = low

    def inverse_factor(buffer, send, recv):
        gram = lax.dot_general(planes[...], planes[...], NT, preferred_element_type=F32)
        gram = gram[:NEV] + gram[NEV:]
        gram = gram[:, :NEV] + gram[:, NEV:]
        buffer[col, :, 0:NEV] = gram[:GV]
        buffer[col, :, LANES // 2:LANES // 2 + NEV] = gram[GV:]
        for slot in all_o:
            gram_copy(buffer, send, recv, slot).start()
        others = buffer.at[pl.ds(0, len(peers_o))]
        remote(others, others, send, recv, (row, index_o(peers_o[0]))).wait()
        total = buffer[0]
        for i in range(1, 8):
            total = total + buffer[i]
        total = jnp.concatenate([total, pltpu.roll(total, LANES // 2, 1)], axis=0)
        work[...] = jnp.where(lane < NEV, total, jnp.where(lane - NEV == sublane, 1.0, 0.0))

        def eliminate(i, carry):
            j = 2 * i
            rest = work[...]
            row_a, row_b = work[pl.ds(j, 1), :], work[pl.ds(j + 1, 1), :]
            at_a, at_b = lane == j, lane == j + 1

            def entry(mask, values):
                return jnp.sum(jnp.where(mask, values, 0.0), axis=1, keepdims=True)

            pivot_a = entry(at_a[0:1], row_a)
            cross = entry(at_b[0:1], row_a) / pivot_a
            pivot_b = entry(at_b[0:1], row_b) - cross * entry(at_b[0:1], row_a)
            column_a, column_b = entry(at_a, rest), entry(at_b, rest)
            row_b = row_b - cross * row_a
            below = sublane[:, 0:1] > j + 1
            factor_a = jnp.where(below, column_a / pivot_a, 0.0)
            factor_b = jnp.where(below, (column_b - cross * column_a) / pivot_b, 0.0)
            updated = rest - factor_a * row_a - factor_b * row_b
            work[...] = jnp.where(sublane == j, row_a * lax.rsqrt(pivot_a), jnp.where(
                sublane == j + 1, row_b * lax.rsqrt(pivot_b), updated))
            return carry

        lax.fori_loop(0, NEV // 2, eliminate, 0)
        return work[:, NEV:2 * NEV]

    def apply_factor(factor, cols_at):
        high, low = split_planes(factor)
        factor_planes = jnp.concatenate([high, low], axis=0)
        total = (jnp.dot(factor_planes, planes[0:NEV, cols_at], preferred_element_type=F32)
                 + jnp.dot(factor_planes, planes[NEV:2 * NEV, cols_at], preferred_element_type=F32))
        return total[:NEV] + total[NEV:]

    factor = inverse_factor(gram_a, g_s, g_r)
    for j in range(0, cols_dev, wide):
        high, low = split_planes(apply_factor(factor, slice(j, j + wide)))
        planes[0:NEV, j:j + wide] = high
        planes[NEV:2 * NEV, j:j + wide] = low
    factor = inverse_factor(gram_b, h_s, h_r)
    for j in range(0, cols_dev, wide):
        out_ref[:, j:j + wide] = apply_factor(factor, slice(j, j + wide))


def on_device(hamilton, start_block, bounds, degree_pick):
    rows_dev, cols_dev = hamilton.shape
    tiles_o = rows_dev // LANES * TPB
    tiles_e = cols_dev // LANES * TPB
    vmem = pltpu.VMEM
    dma = pltpu.SemaphoreType.DMA
    second = pl.pallas_call(
        functools.partial(kernel, (rows_dev, cols_dev)),
        out_shape=jax.ShapeDtypeStruct((NEV, cols_dev), F32),
        in_specs=[
            pl.BlockSpec(memory_space=pl.ANY),
            pl.BlockSpec(memory_space=pl.ANY),
            pl.BlockSpec(memory_space=pltpu.SMEM),
            pl.BlockSpec(memory_space=pltpu.SMEM),
        ],
        out_specs=pl.BlockSpec(memory_space=pltpu.VMEM),
        scratch_shapes=[
            vmem((SLOTS, CHUNK, cols_dev), F32),
            vmem((rows_dev, cols_dev), BF16),
            vmem((rows_dev, cols_dev), BF16),
            vmem((cols_dev, rows_dev), BF16),
            vmem((cols_dev, rows_dev), BF16),
            vmem((2 * NEV, cols_dev), BF16),
            vmem((2 * PADV, cols_dev), BF16),
            vmem((NEV, cols_dev), F32),
            vmem((GROUPS, tiles_o, SUB, LANES), F32),
            vmem((GROUPS, tiles_e, SUB, LANES), F32),
            vmem((GROUPS, 7, FIVE, SUB, LANES), F32),
            vmem((GROUPS, 15, FIVE, SUB, LANES), F32),
            vmem((GROUPS, tiles_o, SUB, LANES), F32),
            vmem((GROUPS, tiles_e, SUB, LANES), F32),
            vmem((GROUPS, FIVE, SUB, LANES), F32),
            vmem((GROUPS, FIVE, SUB, LANES), F32),
            vmem((GROUPS, FIVE, SUB, LANES), F32),
            vmem((NEV // SUB, SUB, LANES), jnp.int32),
            vmem((8, GV, LANES), F32),
            vmem((8, GV, LANES), F32),
            vmem((NEV, LANES), F32),
            dma((SLOTS,)),
            dma,
            dma((GROUPS,)), dma((GROUPS,)), dma((GROUPS,)), dma((GROUPS,)),
            dma((GROUPS,)), dma((GROUPS,)), dma((GROUPS,)), dma((GROUPS,)),
            dma, dma, dma, dma,
        ],
        compiler_params=pltpu.CompilerParams(
            collective_id=0, has_side_effects=True, vmem_limit_bytes=62 * 2**20),
        cost_estimate=pl.CostEstimate(
            flops=2 * DHI * 4 * NEV * rows_dev * cols_dev,
            bytes_accessed=4 * rows_dev * cols_dev, transcendentals=0),
    )(hamilton, start_block, bounds, degree_pick)
    return second * jnp.sqrt(jnp.float32(cols_dev * lax.axis_size("col")))


def solution(mesh):
    in_specs = (P("row", "col"), P(None, "col"), P(), P())
    out_specs = P(None, "col")
    return jax.shard_map(
        on_device, mesh=mesh, in_specs=in_specs, out_specs=out_specs, check_vma=False
    )
```

```python
import functools

import jax
import jax.numpy as jnp
from jax import lax
from jax.experimental import pallas as pl
from jax.experimental.pallas import tpu as pltpu
from jax.sharding import PartitionSpec as P

DLO = 6
DHI = 10
NEV = 48
GROUPS = 2
GV = NEV // GROUPS
PADV = 32
LANES = 128
SUB = 8
TPB = GV // SUB
PAIR = 9
FIVE = 5
FOUR = 4
CHUNK = 256
SLOTS = 4
MESH = pl.DeviceIdType.MESH
NT = (((1,), (1,)), ((), ()))
NN = (((1,), (0,)), ((), ()))
FAR_FIRST = (2, 1, 3, 0)
F32 = jnp.float32
BF16 = jnp.bfloat16


def split_planes(value):
    high = value.astype(BF16)
    low = (value - high.astype(F32)).astype(BF16)
    return high, low


def kernel(
    sizes,
    ham_ref, start_hbm, bounds_ref, pick_ref, out_ref,
    stage, high_ref, low_ref, high_t, low_t, planes, group_planes, start_ref,
    part_o, part_e, land_o, land_e, vec_o, vec_e, last_o, last_e, kept_ref,
    pick_tiles, gram_a, gram_b, work,
    ham_sem, start_sem,
    rs_o_s, rs_o_r, ag_o_s, ag_o_r, rs_e_s, rs_e_r, ag_e_s, ag_e_r,
    g_s, g_r, h_s, h_r,
):
    rows_dev, cols_dev = sizes
    row = lax.axis_index("row")
    col = lax.axis_index("col")
    y, x = row // 4, lax.rem(row, 4)
    z, core = col // 2, lax.rem(col, 2)
    blocks_o, blocks_e = rows_dev // LANES, cols_dev // LANES
    wide = cols_dev // 4
    wide_tiles = wide // LANES * TPB
    odd_row = lax.rem(row, 2)

    peers_o = [(dz, dc) for dz in FAR_FIRST for dc in (0, 1) if (dz, dc) != (0, 0)]
    peers_e = [(dy, dx) for dy in FAR_FIRST for dx in FAR_FIRST if (dy, dx) != (0, 0)]
    all_o, all_e = range(len(peers_o)), range(len(peers_e))

    def index_o(offset):
        return lax.rem(z + offset[0], 4) * 2 + lax.rem(core + offset[1], 2)

    def index_e(offset):
        return lax.rem(y + offset[0], 4) * 4 + lax.rem(x + offset[1], 4)

    def shared(index, parity):
        if parity == 0:
            return pl.ds((index // 2) * PAIR, FIVE)
        return pl.ds((index // 2) * PAIR + FIVE, FOUR)

    def by_parity(odd, act):
        for parity in (0, 1):
            pl.when(odd == parity)(functools.partial(act, parity))

    def landing(land, g, slot, parity):
        return land.at[g, slot] if parity == 0 else land.at[g, slot, pl.ds(1, FOUR)]

    def landing_all(land, g, parity):
        return land.at[g] if parity == 0 else land.at[g, :, pl.ds(1, FOUR)]

    def remote(source, target, send, recv, device):
        return pltpu.make_async_remote_copy(
            src_ref=source, dst_ref=target, send_sem=send, recv_sem=recv,
            device_id=device, device_id_type=MESH)

    def scatter_o(g, slot, parity):
        to = index_o(peers_o[slot])
        return remote(part_o.at[g, shared(to, parity)], landing(land_o, g, slot, parity),
                      rs_o_s.at[g], rs_o_r.at[g], (row, to))

    def scatter_e(g, slot, parity):
        to = index_e(peers_e[slot])
        return remote(part_e.at[g, shared(to, parity)], landing(land_e, g, slot, parity),
                      rs_e_s.at[g], rs_e_r.at[g], (to, col))

    def gather_o(g, slot, parity):
        mine = vec_o.at[g, shared(col, parity)]
        return remote(mine, mine, ag_o_s.at[g], ag_o_r.at[g], (row, index_o(peers_o[slot])))

    def gather_e(g, slot, parity):
        mine = vec_e.at[g, shared(row, parity)]
        return remote(mine, mine, ag_e_s.at[g], ag_e_r.at[g], (index_e(peers_e[slot]), col))

    def partner(parity, offset):
        return (parity + offset[1]) % 2

    def spread(vec, g, value, index, odd, gather, slots):
        def act(parity):
            vec[g, shared(index, parity)] = value[parity:]
            for slot in slots:
                gather(g, slot, parity).start()

        by_parity(odd, act)

    def everything(buffer, g, parity):
        return buffer.at[g, pl.ds(0, buffer.shape[1] - FIVE + parity)]

    def arrived(g, odd, vec, recv):
        def act(parity):
            whole = everything(vec, g, parity)
            remote(whole, whole, recv.at[g], recv.at[g], (row, index_o(peers_o[0]))).wait_recv()

        by_parity(odd, act)

    def left(g, odd, land, send):
        def act(parity):
            whole = landing_all(land, g, parity)
            remote(whole, whole, send.at[g], send.at[g], (row, index_o(peers_o[0]))).wait_send()

        by_parity(odd, act)

    def send_parts(g, odd, scatter, peers, slots):
        def act(parity):
            for slot in slots:
                scatter(g, slot, partner(parity, peers[slot])).start()

        by_parity(odd, act)

    def sent_parts(g, odd, part, send):
        def act(parity):
            whole = everything(part, g, parity)
            remote(whole, whole, send.at[g], send.at[g], (row, index_o(peers_o[0]))).wait_send()

        by_parity(odd, act)

    def parts_here(g, odd, land, recv):
        def act(parity):
            whole = landing_all(land, g, parity)
            remote(whole, whole, recv.at[g], recv.at[g], (row, index_o(peers_o[0]))).wait_recv()

        by_parity(odd, act)

    def summed(index):
        return pl.ds((index // 2) * PAIR + lax.rem(index, 2) * FOUR, FIVE)

    def gram_copy(buffer, send, recv, slot):
        return pltpu.make_async_remote_copy(
            src_ref=buffer.at[col], dst_ref=buffer.at[col],
            send_sem=send, recv_sem=recv,
            device_id=(row, index_o(peers_o[slot])), device_id_type=MESH)

    chunks = rows_dev // CHUNK

    def ham_copy(place):
        return pltpu.make_async_copy(
            ham_ref.at[place * CHUNK:(place + 1) * CHUNK], stage.at[place % SLOTS], ham_sem.at[place % SLOTS])

    start_copy = pltpu.make_async_copy(start_hbm, start_ref, start_sem)
    start_copy.start()
    for place in range(SLOTS):
        ham_copy(place).start()

    for g in range(GROUPS):
        for slot in all_o:
            land_o[g, slot, 0] = jnp.zeros((SUB, LANES), F32)
        for slot in all_e:
            land_e[g, slot, 0] = jnp.zeros((SUB, LANES), F32)
    gram_a[...] = jnp.zeros_like(gram_a)
    gram_b[...] = jnp.zeros_like(gram_b)
    barrier = pltpu.get_barrier_semaphore()
    for offset in peers_o:
        pl.semaphore_signal(barrier, inc=1, device_id=(row, index_o(offset)), device_id_type=MESH)
    for offset in peers_e:
        pl.semaphore_signal(barrier, inc=1, device_id=(index_e(offset), col), device_id_type=MESH)

    lowest = jnp.full((SUB, LANES), bounds_ref[0], F32)
    lower_end = jnp.full((SUB, LANES), bounds_ref[1], F32)
    upper_end = jnp.full((SUB, LANES), bounds_ref[2], F32)
    half_width = (upper_end - lower_end) / 2.0
    center = (upper_end + lower_end) / 2.0
    sigma_one = half_width / (lowest - center)

    tile_shape = (NEV // SUB, SUB, LANES)
    vector_at = lax.broadcasted_iota(jnp.int32, tile_shape, 0) * SUB + lax.broadcasted_iota(
        jnp.int32, tile_shape, 1)
    picked = jnp.zeros(tile_shape, jnp.int32)
    for v in range(NEV):
        picked = jnp.where(vector_at == v, pick_ref[v], picked)
    pick_tiles[...] = picked

    start_copy.wait()
    for b in range(blocks_e):
        value = start_ref[:, b * LANES:(b + 1) * LANES]
        high, low = split_planes(value)
        planes[0:NEV, b * LANES:(b + 1) * LANES] = high
        planes[NEV:2 * NEV, b * LANES:(b + 1) * LANES] = low
        for g in range(GROUPS):
            vec_e[g, b * TPB:(b + 1) * TPB] = value[g * GV:(g + 1) * GV].reshape(TPB, SUB, LANES)
    for g in range(GROUPS):
        last_e[g] = vec_e[g, summed(row)]
    last_o[...] = jnp.zeros_like(last_o)

    offset = row * rows_dev - col * cols_dev
    inside = (offset >= 0) & (offset < cols_dev)
    diag_at = jnp.where(inside, offset, 0)
    diag_weight = jnp.where(inside, 1.0, 0.0).astype(F32)
    eye = (lax.broadcasted_iota(jnp.int32, (LANES, LANES), 0)
           == lax.broadcasted_iota(jnp.int32, (LANES, LANES), 1))
    shift = jnp.where(eye, center[0:1] * diag_weight, 0.0)

    def store_tiles(part, g, first_tile, total):
        for b in range(total.shape[1] // LANES):
            part[g, pl.ds(first_tile + b * TPB, TPB)] = total[:, b * LANES:(b + 1) * LANES].reshape(
                TPB, SUB, LANES)

    def split_chunk(place):
        slot, first_row = place % SLOTS, place * CHUNK
        ham_copy(place).wait()
        for b in range(CHUNK // LANES):
            at = pl.ds(pl.multiple_of(diag_at + first_row + b * LANES, LANES), LANES)
            rows_at = slice(b * LANES, (b + 1) * LANES)
            stage[slot, rows_at, at] = stage[slot, rows_at, at] - shift
        for i in range(0, CHUNK, 16):
            high, low = split_planes(stage[slot, i:i + 16, :])
            high_ref[first_row + i:first_row + i + 16, :] = high
            low_ref[first_row + i:first_row + i + 16, :] = low

    def multiply_chunk(place):
        rows_at = slice(place * CHUNK, (place + 1) * CHUNK)
        total = (lax.dot_general(planes[...], high_ref[rows_at, :], NT, preferred_element_type=F32)
                 + lax.dot_general(planes[...], low_ref[rows_at, :], NT, preferred_element_type=F32))
        total = total[:NEV] + total[NEV:]
        for g in range(GROUPS):
            store_tiles(part_o, g, place * CHUNK // LANES * TPB, total[g * GV:(g + 1) * GV])

    def in_half(offset, half):
        return lax.rem(z + offset[0], 4) // 2 == half

    def slots_at(dz):
        return [slot for slot in all_o if peers_o[slot][0] == dz]

    def send_half(half):
        for g in range(GROUPS):
            for dz in FAR_FIRST:
                pl.when(in_half((dz, 0), half))(
                    functools.partial(send_parts, g, core, scatter_o, peers_o, slots_at(dz)))

    split_chunk(0)
    for place in range(chunks):
        if place + SLOTS < chunks:
            ham_copy(place + SLOTS).start()
        if place + 1 < chunks:
            split_chunk(place + 1)
        multiply_chunk(place)
        if place == chunks // 2 - 1:
            pl.semaphore_wait(barrier, len(peers_o) + len(peers_e))
            send_half(0)
    send_half(1)

    def transpose(piece):
        rows_at = slice(piece * (rows_dev // 4), (piece + 1) * (rows_dev // 4))
        for j in range(0, cols_dev, 512):
            high_t[j:j + 512, rows_at] = high_ref[rows_at, j:j + 512].T
            low_t[j:j + 512, rows_at] = low_ref[rows_at, j:j + 512].T

    def reduce(g, scale, coeff, part, land, last, index, odd, recv, slots):
        parts_here(g, odd, land, recv)
        total = part[g, summed(index)]
        for slot in slots:
            total = total + land[g, slot]
        value = scale * total - coeff * last[g]
        last[g] = value
        return value

    def reduce_o(g, scale, coeff):
        value = reduce(g, scale, coeff, part_o, land_o, last_o, col, core, rs_o_r, all_o)
        spread(vec_o, g, value, col, core, gather_o, all_o)
        sent_parts(g, core, part_o, rs_o_s)

    def reduce_e(g, scale, coeff):
        return reduce(g, scale, coeff, part_e, land_e, last_e, row, odd_row, rs_e_r, all_e)

    def spread_e(g, value):
        spread(vec_e, g, value, row, odd_row, gather_e, all_e)
        sent_parts(g, odd_row, part_e, rs_e_s)

    def to_planes(vec, g, blocks):
        nothing = jnp.zeros((PADV - GV, LANES), F32)
        for b in range(blocks):
            value = vec[g, b * TPB:(b + 1) * TPB].reshape(GV, LANES)
            high, low = split_planes(jnp.concatenate([value, nothing], axis=0))
            group_planes[0:PADV, b * LANES:(b + 1) * LANES] = high
            group_planes[PADV:2 * PADV, b * LANES:(b + 1) * LANES] = low

    def product(depth, high, low, target):
        cols_at = pl.ds(pl.multiple_of(target * wide, LANES), wide)
        vectors = group_planes[:, 0:depth]
        total = (lax.dot_general(vectors, high[:, cols_at], NN, preferred_element_type=F32)
                 + lax.dot_general(vectors, low[:, cols_at], NN, preferred_element_type=F32))
        return total[:GV] + total[PADV:PADV + GV]

    def product_e(g):
        arrived(g, core, vec_o, ag_o_r)
        to_planes(vec_o, g, blocks_o)
        for dy in FAR_FIRST:
            target = lax.rem(y + dy, 4)
            store_tiles(part_e, g, target * wide_tiles, product(rows_dev, high_ref, low_ref, target))
            send_parts(g, odd_row, scatter_e, peers_e, [s for s in all_e if peers_e[s][0] == dy])
        left(g, core, land_o, ag_o_s)

    def product_o(g):
        arrived(g, odd_row, vec_e, ag_e_r)
        to_planes(vec_e, g, blocks_e)
        for other in (1, 0):
            target = lax.rem(z // 2 + other, 2)
            store_tiles(part_o, g, target * wide_tiles, product(cols_dev, high_t, low_t, target))
            for dz in FAR_FIRST:
                pl.when(in_half((dz, 0), target))(
                    functools.partial(send_parts, g, core, scatter_o, peers_o, slots_at(dz)))
        left(g, odd_row, land_e, ag_e_s)

    def next_sigma(sigma):
        new_sigma = 1.0 / (2.0 / sigma_one - sigma)
        return 2.0 * new_sigma / half_width, sigma * new_sigma, new_sigma

    transpose(0)
    transpose(1)
    for g in range(GROUPS):
        reduce_o(g, sigma_one / half_width, 0.0 * sigma_one)
    transpose(2)
    transpose(3)

    def two_steps(pair, sigma):
        scale, coeff, sigma = next_sigma(sigma)
        for g in range(GROUPS):
            product_e(g)
        for g in range(GROUPS):
            value = reduce_e(g, scale, coeff)
            kept_ref[g] = jnp.where(pair == DLO // 2 - 1, value, kept_ref[g])
            spread_e(g, value)
        scale, coeff, sigma = next_sigma(sigma)
        for g in range(GROUPS):
            product_o(g)
        for g in range(GROUPS):
            reduce_o(g, scale, coeff)
        return sigma

    kept_ref[...] = jnp.zeros_like(kept_ref)
    sigma = lax.fori_loop(0, DHI // 2 - 1, two_steps, sigma_one)
    scale, coeff, sigma = next_sigma(sigma)
    for g in range(GROUPS):
        product_e(g)
    first_tile = (row // 2) * PAIR + odd_row * FOUR
    for g in range(GROUPS):
        value = reduce_e(g, scale, coeff)
        degrees = jnp.stack([pick_tiles[g * TPB + lax.rem(first_tile + t, TPB)] for t in range(FIVE)])
        spread_e(g, jnp.where(degrees == 0, kept_ref[g], value))

    for g in range(GROUPS):
        arrived(g, odd_row, vec_e, ag_e_r)
        for b in range(blocks_e):
            cols_at = slice(b * LANES, (b + 1) * LANES)
            start_ref[g * GV:(g + 1) * GV, cols_at] = vec_e[g, b * TPB:(b + 1) * TPB].reshape(GV, LANES)
    for g in range(GROUPS):
        left(g, odd_row, land_e, ag_e_s)

    lane = lax.broadcasted_iota(jnp.int32, (NEV, LANES), 1)
    sublane = lax.broadcasted_iota(jnp.int32, (NEV, LANES), 0)

    high, low = split_planes(start_ref[...])
    planes[0:NEV] = high
    planes[NEV:2 * NEV] = low

    def inverse_factor(buffer, send, recv):
        gram = lax.dot_general(planes[...], planes[...], NT, preferred_element_type=F32)
        gram = gram[:NEV] + gram[NEV:]
        gram = gram[:, :NEV] + gram[:, NEV:]
        buffer[col, :, 0:NEV] = gram[:GV]
        buffer[col, :, LANES // 2:LANES // 2 + NEV] = gram[GV:]
        for slot in all_o:
            gram_copy(buffer, send, recv, slot).start()
        others = buffer.at[pl.ds(0, len(peers_o))]
        remote(others, others, send, recv, (row, index_o(peers_o[0]))).wait()
        total = buffer[0]
        for i in range(1, 8):
            total = total + buffer[i]
        total = jnp.concatenate([total, pltpu.roll(total, LANES // 2, 1)], axis=0)
        work[...] = jnp.where(lane < NEV, total, jnp.where(lane - NEV == sublane, 1.0, 0.0))

        def eliminate(i, carry):
            j = 2 * i
            rest = work[...]
            row_a, row_b = work[pl.ds(j, 1), :], work[pl.ds(j + 1, 1), :]
            at_a, at_b = lane == j, lane == j + 1

            def entry(mask, values):
                return jnp.sum(jnp.where(mask, values, 0.0), axis=1, keepdims=True)

            pivot_a = entry(at_a[0:1], row_a)
            cross = entry(at_b[0:1], row_a) / pivot_a
            pivot_b = entry(at_b[0:1], row_b) - cross * entry(at_b[0:1], row_a)
            column_a, column_b = entry(at_a, rest), entry(at_b, rest)
            row_b = row_b - cross * row_a
            below = sublane[:, 0:1] > j + 1
            factor_a = jnp.where(below, column_a / pivot_a, 0.0)
            factor_b = jnp.where(below, (column_b - cross * column_a) / pivot_b, 0.0)
            updated = rest - factor_a * row_a - factor_b * row_b
            work[...] = jnp.where(sublane == j, row_a * lax.rsqrt(pivot_a), jnp.where(
                sublane == j + 1, row_b * lax.rsqrt(pivot_b), updated))
            return carry

        lax.fori_loop(0, NEV // 2, eliminate, 0)
        return work[:, NEV:2 * NEV]

    def apply_factor(factor, cols_at):
        high, low = split_planes(factor)
        factor_planes = jnp.concatenate([high, low], axis=0)
        total = (jnp.dot(factor_planes, planes[0:NEV, cols_at], preferred_element_type=F32)
                 + jnp.dot(factor_planes, planes[NEV:2 * NEV, cols_at], preferred_element_type=F32))
        return total[:NEV] + total[NEV:]

    factor = inverse_factor(gram_a, g_s, g_r)
    for j in range(0, cols_dev, wide):
        high, low = split_planes(apply_factor(factor, slice(j, j + wide)))
        planes[0:NEV, j:j + wide] = high
        planes[NEV:2 * NEV, j:j + wide] = low
    factor = inverse_factor(gram_b, h_s, h_r)
    for j in range(0, cols_dev, wide):
        out_ref[:, j:j + wide] = apply_factor(factor, slice(j, j + wide))


def on_device(hamilton, start_block, bounds, degree_pick):
    rows_dev, cols_dev = hamilton.shape
    tiles_o = rows_dev // LANES * TPB
    tiles_e = cols_dev // LANES * TPB
    vmem = pltpu.VMEM
    dma = pltpu.SemaphoreType.DMA
    second = pl.pallas_call(
        functools.partial(kernel, (rows_dev, cols_dev)),
        out_shape=jax.ShapeDtypeStruct((NEV, cols_dev), F32),
        in_specs=[
            pl.BlockSpec(memory_space=pl.ANY),
            pl.BlockSpec(memory_space=pl.ANY),
            pl.BlockSpec(memory_space=pltpu.SMEM),
            pl.BlockSpec(memory_space=pltpu.SMEM),
        ],
        out_specs=pl.BlockSpec(memory_space=pltpu.VMEM),
        scratch_shapes=[
            vmem((SLOTS, CHUNK, cols_dev), F32),
            vmem((rows_dev, cols_dev), BF16),
            vmem((rows_dev, cols_dev), BF16),
            vmem((cols_dev, rows_dev), BF16),
            vmem((cols_dev, rows_dev), BF16),
            vmem((2 * NEV, cols_dev), BF16),
            vmem((2 * PADV, cols_dev), BF16),
            vmem((NEV, cols_dev), F32),
            vmem((GROUPS, tiles_o, SUB, LANES), F32),
            vmem((GROUPS, tiles_e, SUB, LANES), F32),
            vmem((GROUPS, 7, FIVE, SUB, LANES), F32),
            vmem((GROUPS, 15, FIVE, SUB, LANES), F32),
            vmem((GROUPS, tiles_o, SUB, LANES), F32),
            vmem((GROUPS, tiles_e, SUB, LANES), F32),
            vmem((GROUPS, FIVE, SUB, LANES), F32),
            vmem((GROUPS, FIVE, SUB, LANES), F32),
            vmem((GROUPS, FIVE, SUB, LANES), F32),
            vmem((NEV // SUB, SUB, LANES), jnp.int32),
            vmem((8, GV, LANES), F32),
            vmem((8, GV, LANES), F32),
            vmem((NEV, LANES), F32),
            dma((SLOTS,)),
            dma,
            dma((GROUPS,)), dma((GROUPS,)), dma((GROUPS,)), dma((GROUPS,)),
            dma((GROUPS,)), dma((GROUPS,)), dma((GROUPS,)), dma((GROUPS,)),
            dma, dma, dma, dma,
        ],
        compiler_params=pltpu.CompilerParams(
            collective_id=0, has_side_effects=True, vmem_limit_bytes=62 * 2**20),
        cost_estimate=pl.CostEstimate(
            flops=2 * DHI * 4 * NEV * rows_dev * cols_dev,
            bytes_accessed=4 * rows_dev * cols_dev, transcendentals=0),
    )(hamilton, start_block, bounds, degree_pick)
    return second * jnp.sqrt(jnp.float32(cols_dev * lax.axis_size("col")))


def solution(mesh):
    in_specs = (P("row", "col"), P(None, "col"), P(), P())
    out_specs = P(None, "col")
    return jax.shard_map(
        on_device, mesh=mesh, in_specs=in_specs, out_specs=out_specs, check_vma=False
    )
```
